256 devices in a mesh: strike: 32 (over z, y_hi, core), cross: 8 (over x, y_lo).
Axes of the slice: x: 4, y: 4 (y_hi: 2, y_lo: 2; y = y_hi * 2 + y_lo), z: 8, core: 2. Of those that a mesh axis runs over, the one named last changes fastest.
Arguments:
- velocity: float32 [3, 512, 128, 256], P(None, 'strike', 'cross'), may hold values from -4 to 4
- stress: float32 [6, 512, 128, 256], P(None, 'strike', 'cross'), may hold values from -1.6 to 1.6
- buoyancy: float32 [512, 128, 256], P('strike', 'cross'), may hold values from 0.5 to 1
- lame: float32 [512, 128, 256], P('strike', 'cross'), may hold values from 0.5 to 1.2
- shear: float32 [512, 128, 256], P('strike', 'cross'), may hold values from 0.5 to 1
- fault_tile: int32 [32], replicated, may hold values from 1 to 7
- prestress: float32 [512, 256], P('strike', 'cross'), may hold values from 1.2 to 2.4
- normal_stress: float32 [512, 256], P('strike', 'cross'), may hold values from 2 to 4
- rate_a: float32 [512, 256], P('strike', 'cross'), may hold values from 0.02 to 0.04
- state: float32 [512, 256], P('strike', 'cross'), may hold values from 0.45 to 0.6
Outputs:
- velocity_out: float32 [3, 512, 128, 256], P(None, 'strike', 'cross')
- stress_out: float32 [6, 512, 128, 256], P(None, 'strike', 'cross')
- slip_rate: float32 [512, 256], P('strike', 'cross')
- state_out: float32 [512, 256], P('strike', 'cross')
The draws below stay inside these ranges and needn't reach their ends.
Inputs may be any that keep to these rules, and one draw needn't show every extreme that they name: `fault_tile`: each strike index has its fault plane in the first row of one cross tile other than the first.
All inputs are finite; a program needn't handle non-finite values.
Results may differ from the reference program's by a relative error of at most 0.0003.
Values sent between devices are 32-bit elements; how exact they have to be, the bound alone decides.
A program may use at most 64 MiB of HBM per device.

```python
import math
import jax
import jax.numpy as jnp

CX = 16
CY = 16
NZ = 256
STEPS = 4
NEWTON = 8
NX = 512
NY = 128
N_STRIKE = 32
N_CROSS = 8


def touch_ends(array, own_key, low, largest):
    index_at = [jax.random.randint(jax.random.fold_in(own_key, axis), (), 0, length) for axis, length in enumerate(array.shape)]
    widest = array.shape.index(max(array.shape))
    neighbour = index_at[:widest] + [(index_at[widest] + 1) % array.shape[widest]] + index_at[widest + 1:]
    return array.at[tuple(index_at)].set(low).at[tuple(neighbour)].set(largest)


def levels(stream_key, extent, split, least, top_value):
    def one(dim, blocks):
        steps = jax.random.uniform(jax.random.fold_in(jax.random.fold_in(stream_key, 6), dim), (blocks,), jnp.float32, least / len(split), top_value / len(split))
        return jnp.repeat(jnp.exp(steps), extent[dim] // blocks).reshape((-1,) + (1,) * (len(extent) - dim - 1))

    gain = one(*split[0])
    for cut in split[1:]:
        gain = gain * one(*cut)
    return gain


def noise(own_key, dims, scale, most, shards=(), held_as=jnp.bfloat16):
    entries = scale * jax.random.normal(own_key, dims, jnp.float32)
    if shards:
        entries = entries * levels(own_key, dims, shards, -0.22, 0.18)
    return jnp.clip(entries, -most, most).astype(held_as)


def setup_inputs(seed: int = 0) -> dict:
    key_list = jax.random.split(jax.random.key(seed), 11)
    velocity = noise(key_list[0], (3, NX, NY, NZ), 0.5, 4.0, ((1, 32), (2, 8)), jnp.float32)
    stress = noise(key_list[1], (6, NX, NY, NZ), 0.2, 1.6, ((1, 32), (2, 8)), jnp.float32)
    buoyancy = jnp.clip(0.5 + 0.5 * jax.random.uniform(key_list[2], (NX, NY, NZ), jnp.float32) ** levels(key_list[2], (NX, NY, NZ), ((0, 32), (1, 8)), -0.2, 0.2), 0.5, 1.0)
    lame = jnp.clip(0.5 + 0.70000005 * jax.random.uniform(key_list[3], (NX, NY, NZ), jnp.float32) ** levels(key_list[3], (NX, NY, NZ), ((0, 32), (1, 8)), -0.2, 0.2), 0.5, 1.2)
    shear = jnp.clip(0.5 + 0.5 * jax.random.uniform(key_list[4], (NX, NY, NZ), jnp.float32) ** levels(key_list[4], (NX, NY, NZ), ((0, 32), (1, 8)), -0.2, 0.2), 0.5, 1.0)
    fault_tile = touch_ends(jax.random.randint(key_list[5], (N_STRIKE,), 1, N_CROSS), jax.random.fold_in(key_list[5], 1), 1, N_CROSS - 1).astype(jnp.int32)
    prestress = jnp.clip(1.2 + 1.2 * jax.random.uniform(key_list[6], (NX, NZ), jnp.float32) ** levels(key_list[6], (NX, NZ), ((0, 32), (1, 8)), -0.2, 0.2), 1.2, 2.4)
    normal_stress = jnp.clip(jnp.exp(math.log(4.0) - 0.6931472 * jax.random.uniform(key_list[7], (NX, NZ), jnp.float32) ** levels(key_list[7], (NX, NZ), ((0, 32), (1, 8)), -0.2, 0.2)), 2.0, 4.0)
    rate_a = jnp.clip(jnp.exp(math.log(0.04) - 0.6931472 * jax.random.uniform(key_list[8], (NX, NZ), jnp.float32) ** levels(key_list[8], (NX, NZ), ((0, 32), (1, 8)), -0.2, 0.2)), 0.02, 0.04)
    state = jnp.clip(0.45 + 0.15000004 * jax.random.uniform(key_list[9], (NX, NZ), jnp.float32) ** levels(key_list[9], (NX, NZ), ((0, 32), (1, 8)), -0.2, 0.2), 0.45, 0.6)
    return dict(velocity=velocity, stress=stress, buoyancy=buoyancy, lame=lame, shear=shear, fault_tile=fault_tile, prestress=prestress, normal_stress=normal_stress, rate_a=rate_a, state=state)


step_ratio = 0.25
ref_rate = 0.001
evolve_rate = 1e-05
base_friction = 0.6
evolve_b = 0.03

def inverse_sinh(value):
    magnitude = jnp.abs(value)
    return jnp.sign(value) * jnp.log(magnitude + jnp.sqrt(magnitude * magnitude + 1.0))

def shifted(field, axis_pos, offset):
    parts = [slice(2, field.shape[position] - 2) for position in range(3)]
    parts[axis_pos] = slice(2 + offset, field.shape[axis_pos] - 2 + offset)
    return field[tuple(parts)]

def forward_diff(field, axis_pos):
    return 1.125 * (shifted(field, axis_pos, 1) - shifted(field, axis_pos, 0)) - (shifted(field, axis_pos, 2) - shifted(field, axis_pos, -1)) / 24.0

def backward_diff(field, axis_pos):
    return 1.125 * (shifted(field, axis_pos, 0) - shifted(field, axis_pos, -1)) - (shifted(field, axis_pos, 1) - shifted(field, axis_pos, -2)) / 24.0

def velocity_update(velocity, padded, buoyancy):
    strike_force = forward_diff(padded[0], 0) + backward_diff(padded[3], 1) + backward_diff(padded[4], 2)
    cross_force = backward_diff(padded[3], 0) + forward_diff(padded[1], 1) + backward_diff(padded[5], 2)
    depth_force = backward_diff(padded[4], 0) + backward_diff(padded[5], 1) + forward_diff(padded[2], 2)
    return velocity + step_ratio * buoyancy * jnp.stack([strike_force, cross_force, depth_force])

def stress_update(stress, padded, lame, shear):
    stretch_strike = backward_diff(padded[0], 0)
    stretch_cross = backward_diff(padded[1], 1)
    stretch_depth = backward_diff(padded[2], 2)
    dilation = stretch_strike + stretch_cross + stretch_depth
    normal = jnp.stack([lame * dilation + 2.0 * shear * stretch_strike, lame * dilation + 2.0 * shear * stretch_cross, lame * dilation + 2.0 * shear * stretch_depth])
    tangent = shear * jnp.stack([forward_diff(padded[0], 1) + forward_diff(padded[1], 0), forward_diff(padded[0], 2) + forward_diff(padded[2], 0), forward_diff(padded[1], 2) + forward_diff(padded[2], 1)])
    return stress + step_ratio * jnp.concatenate([normal, tangent], 0)

def friction(trial, damping, prestress, normal_stress, rate_a, state):
    total = trial + prestress
    width = 2.0 * ref_rate * jnp.exp(-state / rate_a)
    strength = rate_a * normal_stress
    scaled = inverse_sinh(total / (damping * width))
    for iteration in range(NEWTON):
        residual = strength * scaled + damping * width * jnp.sinh(scaled) - total
        slope = strength + damping * width * jnp.cosh(scaled)
        scaled = scaled - residual / slope
    slip = width * jnp.sinh(scaled)
    traction = total - damping * slip
    evolved = state + evolve_rate * (jnp.exp((base_friction - state) / evolve_b) - jnp.abs(slip) / ref_rate)
    return (traction - prestress, slip, evolved)

def pad_all(field):
    return jnp.pad(field, ((0, 0), (2, 2), (2, 2), (2, 2)))

def reference(velocity, stress, buoyancy, lame, shear, fault_tile, prestress, normal_stress, rate_a, state):
    columns = jnp.arange(NX, dtype=jnp.int32)
    planes = (fault_tile[columns // CX] * CY).astype(jnp.int32)
    damping = 0.5 * jnp.sqrt(shear[columns, planes, :] / buoyancy[columns, planes, :])
    slip = jnp.zeros((NX, NZ), jnp.float32)
    for iteration in range(STEPS):
        velocity = velocity_update(velocity, pad_all(stress), buoyancy)
        stress = stress_update(stress, pad_all(velocity), lame, shear)
        trial = stress[3, columns, planes, :]
        change, slip, state = friction(trial, damping, prestress, normal_stress, rate_a, state)
        stress = stress.at[3, columns, planes, :].set(change)
    return (velocity, stress, slip, state)
```

```python
import jax
import jax.numpy as jnp
from jax import lax
from jax.experimental import pallas as pl
from jax.experimental.pallas import tpu as pltpu
from jax.sharding import PartitionSpec as P

STEPS = 4
NEWTON = 8

step_ratio = 0.25
ref_rate = 0.001
evolve_rate = 1e-05
base_friction = 0.6
evolve_b = 0.03

CX = 16
CY = 16
NZ = 256
MESH = pl.DeviceIdType.MESH

XX, XZ, XY, YZ, YY, ZZ = range(6)
STRESS_ORDER = (0, 4, 3, 5, 1, 2)
VX, VZ, VY = range(3)
VELOCITY_ORDER = (0, 2, 1)

NEAR = step_ratio * 1.125
FAR = step_ratio / 24.0

RUNS = ((0, 4), (12, 4), (4, 8))


def wave_kernel(
    stress_in,
    velocity_in,
    buoyancy_in,
    lame_in,
    shear_in,
    fault_tile,
    prestress,
    normal_stress,
    rate_a,
    state,
    velocity_out,
    stress_out,
    slip_out,
    state_out,
    stress,
    velocity,
    stress_halo,
    velocity_halo,
    buoyancy,
    lame,
    shear,
    trial,
    ratio,
    fault,
    packed,
    result,
    send_sem,
    recv_sem,
    pack_send,
    pack_recv,
    result_send,
    result_recv,
    load_sem,
    store_sem,
):
    strike = lax.axis_index("strike")
    cross = lax.axis_index("cross")
    n_strike = lax.axis_size("strike")
    n_cross = lax.axis_size("cross")
    has = {
        "up": strike + 1 < n_strike,
        "down": strike >= 1,
        "right": cross + 1 < n_cross,
        "left": cross >= 1,
    }
    place = {
        "up": (strike + 1, cross),
        "down": (strike - 1, cross),
        "right": (strike, cross + 1),
        "left": (strike, cross - 1),
    }
    opposite = {"up": "down", "down": "up", "right": "left", "left": "right"}

    loads = []
    for index, comp in enumerate(STRESS_ORDER):
        loads.append((stress_in.at[comp], stress.at[index, pl.ds(2, CX)]))
    loads.append((buoyancy_in, buoyancy))
    for index, comp in enumerate(VELOCITY_ORDER):
        loads.append((velocity_in.at[comp], velocity.at[index, pl.ds(2, CX)]))
    loads.append((lame_in, lame))
    loads.append((shear_in, shear))
    loads = [
        pltpu.make_async_copy(source, target, load_sem.at[index])
        for index, (source, target) in enumerate(loads)
    ]
    for copy in loads:
        copy.start()

    zero_slab = jnp.zeros((CY, NZ), jnp.float32)
    for index in range(3):
        for slab in (0, 1, 18, 19):
            stress[index, slab] = zero_slab
            velocity[index, slab] = zero_slab

    def clear(slab, carry):
        for index in range(3):
            stress_halo[index, slab] = zero_slab
            velocity_halo[index, slab] = zero_slab
        return carry

    lax.fori_loop(0, CX, clear, 0)

    for index, ref in enumerate((prestress, normal_stress, rate_a, state)):
        value = ref[...]
        columns = pl.ds(32 * index, 32)
        packed[cross, 0:4, columns] = value[0:4]
        packed[cross, 4:8, columns] = value[12:16]
        packed[cross, 8:16, columns] = value[4:12]

    barrier = pltpu.get_barrier_semaphore()
    for side in ("up", "down"):

        @pl.when(has[side])
        def _(side=side):
            pl.semaphore_signal(barrier, inc=1, device_id=place[side], device_id_type=MESH)

    for step in range(1, 8):
        other = lax.rem(cross + step, n_cross)
        pl.semaphore_signal(barrier, inc=1, device_id=(strike, other), device_id_type=MESH)
    pl.semaphore_wait(
        barrier, 7 + has["up"].astype(jnp.int32) + has["down"].astype(jnp.int32)
    )

    def remote(phase, index, side, source, target):
        return (
            side,
            pltpu.make_async_remote_copy(
                src_ref=source,
                dst_ref=target,
                send_sem=send_sem.at[phase, index],
                recv_sem=recv_sem.at[phase, index],
                device_id=place[side],
                device_id_type=MESH,
            ),
        )

    def stress_strike():
        return [
            remote(0, 0, "up", stress.at[1:3, 16:18], stress.at[1:3, 0:2]),
            remote(0, 1, "up", stress.at[0:1, 17:18], stress.at[0:1, 1:2]),
            remote(0, 2, "down", stress.at[1:3, 2:3], stress.at[1:3, 18:19]),
            remote(0, 3, "down", stress.at[0:1, 2:4], stress.at[0:1, 18:20]),
        ]

    def velocity_strike():
        return [
            remote(1, 0, "up", velocity.at[0:1, 16:18], velocity.at[0:1, 0:2]),
            remote(1, 1, "up", velocity.at[1:3, 17:18], velocity.at[1:3, 1:2]),
            remote(1, 2, "down", velocity.at[0:1, 2:3], velocity.at[0:1, 18:19]),
            remote(1, 3, "down", velocity.at[1:3, 2:4], velocity.at[1:3, 18:20]),
        ]

    def stress_cross(run):
        first, count = RUNS[run]
        own, halo = pl.ds(2 + first, count), pl.ds(first, count)
        base = 4 + 4 * run
        return [
            remote(
                0, base, "right", stress.at[2:4, own, 14:16], stress_halo.at[0:2, halo, 14:16]
            ),
            remote(
                0, base + 1, "right", stress.at[4:5, own, 15:16], stress_halo.at[2:3, halo, 15:16]
            ),
            remote(
                0, base + 2, "left", stress.at[2:4, own, 0:1], stress_halo.at[0:2, halo, 0:1]
            ),
            remote(
                0, base + 3, "left", stress.at[4:5, own, 0:2], stress_halo.at[2:3, halo, 0:2]
            ),
        ]

    def velocity_cross(run):
        first, count = RUNS[run]
        own, halo = pl.ds(2 + first, count), pl.ds(first, count)
        base = 4 + 4 * run
        return [
            remote(
                1, base, "right", velocity.at[2:3, own, 14:16], velocity_halo.at[2:3, halo, 14:16]
            ),
            remote(
                1,
                base + 1,
                "right",
                velocity.at[0:2, own, 15:16],
                velocity_halo.at[0:2, halo, 15:16],
            ),
            remote(
                1, base + 2, "left", velocity.at[2:3, own, 0:1], velocity_halo.at[2:3, halo, 0:1]
            ),
            remote(
                1, base + 3, "left", velocity.at[0:2, own, 0:2], velocity_halo.at[0:2, halo, 0:2]
            ),
        ]

    def start(copies):
        for side, copy in copies:

            @pl.when(has[side])
            def _(copy=copy):
                copy.start()

    def wait_recv(copies):
        for side, copy in copies:

            @pl.when(has[opposite[side]])
            def _(copy=copy):
                copy.wait_recv()

    def wait_send(copies):
        for side, copy in copies:

            @pl.when(has[side])
            def _(copy=copy):
                copy.wait_send()

    for copy in loads[:6]:
        copy.wait()
    start(stress_strike() + stress_cross(0) + stress_cross(1) + stress_cross(2))

    def pack_copy(step):
        other = lax.rem(cross + step, n_cross)
        return pltpu.make_async_remote_copy(
            src_ref=packed.at[cross],
            dst_ref=packed.at[cross],
            send_sem=pack_send.at[step],
            recv_sem=pack_recv.at[step],
            device_id=(strike, other),
            device_id_type=MESH,
        )

    for step in range(1, 8):
        pack_copy(step).start()

    for copy in loads[6:]:
        copy.wait()

    row = lax.broadcasted_iota(jnp.int32, (CY, NZ), 0)
    lane = lax.broadcasted_iota(jnp.int32, (CY, NZ), 1)

    def depth(value, offset):
        moved = pltpu.roll(value, (-offset) % NZ, 1)
        if offset < 0:
            return jnp.where(lane < -offset, 0.0, moved)
        return jnp.where(lane >= NZ - offset, 0.0, moved)

    def across(value, halo, offset):
        if offset < 0:
            joined = jnp.where(row >= CY + offset, halo, value)
        else:
            joined = jnp.where(row < offset, halo, value)
        return pltpu.roll(joined, (-offset) % CY, 0)

    def forward_depth(value):
        return (
            depth(value, 1) - value,
            depth(value, 2) - depth(value, -1),
        )

    def backward_depth(value):
        return (
            value - depth(value, -1),
            depth(value, 1) - depth(value, -2),
        )

    def forward_across(value, halo):
        return (
            across(value, halo, 1) - value,
            across(value, halo, 2) - across(value, halo, -1),
        )

    def backward_across(value, halo):
        return (
            value - across(value, halo, -1),
            across(value, halo, 1) - across(value, halo, -2),
        )

    def forward_strike(ref, comp, slab):
        return (
            ref[comp, slab + 1] - ref[comp, slab],
            ref[comp, slab + 2] - ref[comp, slab - 1],
        )

    def backward_strike(ref, comp, slab):
        return (
            ref[comp, slab] - ref[comp, slab - 1],
            ref[comp, slab + 1] - ref[comp, slab - 2],
        )

    def combine(*pairs):
        near, far = pairs[0]
        for pair in pairs[1:]:
            near, far = near + pair[0], far + pair[1]
        return NEAR * near - FAR * far

    def velocity_slab(x):
        slab = x + 2
        b = buoyancy[x]
        xy, yz, yy = stress[XY, slab], stress[YZ, slab], stress[YY, slab]
        xz, zz = stress[XZ, slab], stress[ZZ, slab]
        velocity[VX, slab] += b * combine(
            forward_strike(stress, XX, slab),
            backward_across(xy, stress_halo[0, x]),
            backward_depth(xz),
        )
        velocity[VY, slab] += b * combine(
            backward_strike(stress, XY, slab),
            forward_across(yy, stress_halo[2, x]),
            backward_depth(yz),
        )
        velocity[VZ, slab] += b * combine(
            backward_strike(stress, XZ, slab),
            backward_across(yz, stress_halo[1, x]),
            forward_depth(zz),
        )

    def stress_slab(x, r):
        slab = x + 2
        mu, la = shear[x], lame[x]
        vx, vy, vz = velocity[VX, slab], velocity[VY, slab], velocity[VZ, slab]
        hx, hz, hy = velocity_halo[0, x], velocity_halo[1, x], velocity_halo[2, x]
        ex = combine(backward_strike(velocity, VX, slab))
        ey = combine(backward_across(vy, hy))
        ez = combine(backward_depth(vz))
        spread = la * (ex + ey + ez)
        twice = 2.0 * mu
        stress[XX, slab] += spread + twice * ex
        stress[YY, slab] += spread + twice * ey
        stress[ZZ, slab] += spread + twice * ez
        sheared = stress[XY, slab] + mu * combine(
            forward_across(vx, hx), forward_strike(velocity, VY, slab)
        )
        stress[XY, slab] = sheared
        trial[pl.ds(r, 1), :] = sheared[0:1]
        stress[XZ, slab] += mu * combine(
            forward_depth(vx), forward_strike(velocity, VZ, slab)
        )
        stress[YZ, slab] += mu * combine(forward_depth(vy), forward_across(vz, hz))

    def outer(i):
        return i + jnp.where(i >= 4, 8, 0)

    def velocity_outer(i, carry):
        velocity_slab(outer(i))
        return carry

    def velocity_inner(i, carry):
        velocity_slab(i + 4)
        return carry

    def stress_outer(i, carry):
        stress_slab(outer(i), i)
        return carry

    def stress_inner(i, carry):
        stress_slab(i + 4, i + 8)
        return carry

    owner = fault_tile[strike]
    is_owner = owner == cross
    strike_of = (0, 1, 2, 3, 12, 13, 14, 15, 4, 5, 6, 7, 8, 9, 10, 11)

    for r, x in enumerate(strike_of):
        fault[0, r : r + 1, :] = shear[x, 0:1, :]
        ratio[r : r + 1, :] = buoyancy[x, 0:1, :]
    fault[0] = 0.5 * jnp.sqrt(fault[0] / ratio[...])

    def unpack():
        for step in range(1, 8):
            pack_copy(step).wait_recv()
        part = lax.broadcasted_iota(jnp.int32, (CX, 128), 1) // 32
        for half in range(2):
            blocks = [packed[4 * half + j] for j in range(4)]
            for index in range(4):
                value = None
                for j in range(4):
                    amount = (32 * (j - index)) % 128
                    moved = pltpu.roll(blocks[j], amount, 1) if amount else blocks[j]
                    value = moved if value is None else jnp.where(part == j, moved, value)
                fault[1 + index, :, 128 * half : 128 * half + 128] = value

    def friction(half):
        rows = slice(8 * half, 8 * half + 8)
        damping, before = fault[0, rows], fault[1, rows]
        a, psi = fault[3, rows], fault[4, rows]
        start_value = trial[rows]
        total = start_value + before
        width = 2.0 * ref_rate * jnp.exp(-psi / a)
        strength = a * fault[2, rows]
        scale = damping * width
        argument = total / scale
        magnitude = jnp.abs(argument)
        log = jnp.log(magnitude + jnp.sqrt(magnitude * magnitude + 1.0))
        u = jnp.where(argument < 0.0, -log, log)
        half_scale = 0.5 * scale
        for _ in range(NEWTON):
            grow, shrink = half_scale * jnp.exp(u), half_scale * jnp.exp(-u)
            u = u - (strength * u + (grow - shrink) - total) / (strength + (grow + shrink))
        slip = width * (0.5 * (jnp.exp(u) - jnp.exp(-u)))
        change = total - damping * slip - before
        fault[4, rows] = psi + evolve_rate * (
            jnp.exp((base_friction - psi) / evolve_b) - jnp.abs(slip) / ref_rate
        )
        fault[5, rows] = slip
        update = jnp.where(is_owner, change, start_value)
        for i in range(8):
            stress[XY, 2 + strike_of[8 * half + i], 0:1, :] = update[i : i + 1]

    def step_body(step, carry):
        wait_recv(stress_strike() + stress_cross(0) + stress_cross(1))

        @pl.when(step > 0)
        def _():
            wait_send(velocity_strike() + velocity_cross(0) + velocity_cross(1))

        lax.fori_loop(0, 8, velocity_outer, 0)
        start(velocity_strike() + velocity_cross(0) + velocity_cross(1))
        wait_recv(stress_cross(2))

        @pl.when(step > 0)
        def _():
            wait_send(velocity_cross(2))

        lax.fori_loop(0, 8, velocity_inner, 0)
        start(velocity_cross(2))

        @pl.when(step == 0)
        def _():
            unpack()

        wait_recv(velocity_strike() + velocity_cross(0) + velocity_cross(1))
        wait_send(stress_strike() + stress_cross(0) + stress_cross(1))
        lax.fori_loop(0, 8, stress_outer, 0)
        friction(0)

        @pl.when(step < STEPS - 1)
        def _():
            start(stress_strike() + stress_cross(0) + stress_cross(1))

        wait_recv(velocity_cross(2))
        wait_send(stress_cross(2))
        lax.fori_loop(0, 8, stress_inner, 0)
        friction(1)

        @pl.when(step < STEPS - 1)
        def _():
            start(stress_cross(2))

        return carry

    lax.fori_loop(0, STEPS, step_body, 0)
    wait_send(velocity_strike() + velocity_cross(0) + velocity_cross(1) + velocity_cross(2))

    for half in range(2):
        for j in range(4):
            lanes = slice(128 * half, 128 * half + 128)
            slip_part, state_part = fault[5, :, lanes], fault[4, :, lanes]
            first = pltpu.roll(slip_part, (128 - 32 * j) % 128, 1) if j else slip_part
            second = pltpu.roll(state_part, (160 - 32 * j) % 128, 1) if j != 1 else state_part
            part = lax.broadcasted_iota(jnp.int32, (CX, 128), 1)
            result[0, 4 * half + j] = jnp.where(part < 32, first, second)

    def result_copy(step):
        other = lax.rem(cross + step, n_cross)
        return pltpu.make_async_remote_copy(
            src_ref=result.at[0, other],
            dst_ref=result.at[1, cross],
            send_sem=result_send.at[step],
            recv_sem=result_recv.at[step],
            device_id=(strike, other),
            device_id_type=MESH,
        )

    for step in range(1, 8):
        result_copy(step).start()
    result[1, cross] = result[0, cross]

    stores = []
    for index, comp in enumerate(STRESS_ORDER):
        stores.append((stress.at[index, pl.ds(2, CX)], stress_out.at[comp]))
    for index, comp in enumerate(VELOCITY_ORDER):
        stores.append((velocity.at[index, pl.ds(2, CX)], velocity_out.at[comp]))
    stores = [
        pltpu.make_async_copy(source, target, store_sem.at[index])
        for index, (source, target) in enumerate(stores)
    ]
    for copy in stores:
        copy.start()
    for step in range(1, 8):
        result_copy(step).wait_recv()
    block = result[1, owner]
    for ref, first in ((slip_out, 0), (state_out, 32)):
        value = block[:, first : first + 32]
        ref[0:4] = value[0:4]
        ref[12:16] = value[4:8]
        ref[4:12] = value[8:16]
    for step in range(1, 8):
        pack_copy(step).wait_send()
        result_copy(step).wait_send()
    for copy in stores:
        copy.wait()


def local(
    velocity, stress, buoyancy, lame, shear, fault_tile, prestress, normal_stress, rate_a, state
):
    anywhere = pl.BlockSpec(memory_space=pl.ANY)
    vmem = pl.BlockSpec(memory_space=pltpu.VMEM)
    smem = pl.BlockSpec(memory_space=pltpu.SMEM)
    f32 = jnp.float32
    return pl.pallas_call(
        wave_kernel,
        out_shape=(
            jax.ShapeDtypeStruct(velocity.shape, f32),
            jax.ShapeDtypeStruct(stress.shape, f32),
            jax.ShapeDtypeStruct(state.shape, f32),
            jax.ShapeDtypeStruct(state.shape, f32),
        ),
        in_specs=[anywhere] * 5 + [smem] + [vmem] * 4,
        out_specs=(anywhere, anywhere, vmem, vmem),
        scratch_shapes=[
            pltpu.VMEM((6, CX + 4, CY, NZ), f32),
            pltpu.VMEM((3, CX + 4, CY, NZ), f32),
            pltpu.VMEM((3, CX, CY, NZ), f32),
            pltpu.VMEM((3, CX, CY, NZ), f32),
            pltpu.VMEM((CX, CY, NZ), f32),
            pltpu.VMEM((CX, CY, NZ), f32),
            pltpu.VMEM((CX, CY, NZ), f32),
            pltpu.VMEM((CX, NZ), f32),
            pltpu.VMEM((CX, NZ), f32),
            pltpu.VMEM((6, CX, NZ), f32),
            pltpu.VMEM((8, CX, 128), f32),
            pltpu.VMEM((2, 8, CX, 128), f32),
            pltpu.SemaphoreType.DMA((2, 16)),
            pltpu.SemaphoreType.DMA((2, 16)),
            pltpu.SemaphoreType.DMA((8,)),
            pltpu.SemaphoreType.DMA((8,)),
            pltpu.SemaphoreType.DMA((8,)),
            pltpu.SemaphoreType.DMA((8,)),
            pltpu.SemaphoreType.DMA((12,)),
            pltpu.SemaphoreType.DMA((9,)),
        ],
        compiler_params=pltpu.CompilerParams(
            collective_id=0, has_side_effects=True, vmem_limit_bytes=48 * 2**20
        ),
    )(
        stress,
        velocity,
        buoyancy,
        lame,
        shear,
        fault_tile,
        prestress,
        normal_stress,
        rate_a,
        state,
    )


def solution(mesh):
    in_specs = (
        P(None, "strike", "cross", None),
        P(None, "strike", "cross", None),
        P("strike", "cross", None),
        P("strike", "cross", None),
        P("strike", "cross", None),
        P(),
        P("strike", "cross"),
        P("strike", "cross"),
        P("strike", "cross"),
        P("strike", "cross"),
    )
    out_specs = (
        P(None, "strike", "cross", None),
        P(None, "strike", "cross", None),
        P("strike", "cross"),
        P("strike", "cross"),
    )
    return jax.shard_map(local, mesh=mesh, in_specs=in_specs, out_specs=out_specs, check_vma=False)
```

```python
import jax
import jax.numpy as jnp
from jax import lax
from jax.experimental import pallas as pl
from jax.experimental.pallas import tpu as pltpu
from jax.sharding import PartitionSpec as P

STEPS = 4
NEWTON = 8

step_ratio = 0.25
ref_rate = 0.001
evolve_rate = 1e-05
base_friction = 0.6
evolve_b = 0.03

CX = 16
CY = 16
NZ = 256
MESH = pl.DeviceIdType.MESH

XX, XZ, XY, YZ, YY, ZZ = range(6)
STRESS_ORDER = (0, 4, 3, 5, 1, 2)
VX, VZ, VY = range(3)
VELOCITY_ORDER = (0, 2, 1)

NEAR = step_ratio * 1.125
FAR = step_ratio / 24.0

RUNS = ((0, 4), (12, 4), (4, 8))


def wave_kernel(
    stress_in,
    velocity_in,
    buoyancy_in,
    lame_in,
    shear_in,
    fault_tile,
    prestress,
    normal_stress,
    rate_a,
    state,
    velocity_out,
    stress_out,
    slip_out,
    state_out,
    stress,
    velocity,
    stress_halo,
    velocity_halo,
    buoyancy,
    lame,
    shear,
    trial,
    ratio,
    fault,
    packed,
    result,
    send_sem,
    recv_sem,
    pack_send,
    pack_recv,
    result_send,
    result_recv,
    load_sem,
    store_sem,
):
    strike = lax.axis_index("strike")
    cross = lax.axis_index("cross")
    n_strike = lax.axis_size("strike")
    n_cross = lax.axis_size("cross")
    has = {
        "up": strike + 1 < n_strike,
        "down": strike >= 1,
        "right": cross + 1 < n_cross,
        "left": cross >= 1,
    }
    place = {
        "up": (strike + 1, cross),
        "down": (strike - 1, cross),
        "right": (strike, cross + 1),
        "left": (strike, cross - 1),
    }
    opposite = {"up": "down", "down": "up", "right": "left", "left": "right"}

    loads = []
    for index, comp in enumerate(STRESS_ORDER):
        loads.append((stress_in.at[comp], stress.at[index, pl.ds(2, CX)]))
    loads.append((buoyancy_in, buoyancy))
    for index, comp in enumerate(VELOCITY_ORDER):
        loads.append((velocity_in.at[comp], velocity.at[index, pl.ds(2, CX)]))
    loads.append((lame_in, lame))
    loads.append((shear_in, shear))
    loads = [
        pltpu.make_async_copy(source, target, load_sem.at[index])
        for index, (source, target) in enumerate(loads)
    ]
    for copy in loads:
        copy.start()

    zero_slab = jnp.zeros((CY, NZ), jnp.float32)
    for index in range(3):
        for slab in (0, 1, 18, 19):
            stress[index, slab] = zero_slab
            velocity[index, slab] = zero_slab

    def clear(slab, carry):
        for index in range(3):
            stress_halo[index, slab] = zero_slab
            velocity_halo[index, slab] = zero_slab
        return carry

    lax.fori_loop(0, CX, clear, 0)

    for index, ref in enumerate((prestress, normal_stress, rate_a, state)):
        value = ref[...]
        columns = pl.ds(32 * index, 32)
        packed[cross, 0:4, columns] = value[0:4]
        packed[cross, 4:8, columns] = value[12:16]
        packed[cross, 8:16, columns] = value[4:12]

    barrier = pltpu.get_barrier_semaphore()
    for side in ("up", "down"):

        @pl.when(has[side])
        def _(side=side):
            pl.semaphore_signal(barrier, inc=1, device_id=place[side], device_id_type=MESH)

    for step in range(1, 8):
        other = lax.rem(cross + step, n_cross)
        pl.semaphore_signal(barrier, inc=1, device_id=(strike, other), device_id_type=MESH)
    pl.semaphore_wait(
        barrier, 7 + has["up"].astype(jnp.int32) + has["down"].astype(jnp.int32)
    )

    def remote(phase, index, side, source, target):
        return (
            side,
            pltpu.make_async_remote_copy(
                src_ref=source,
                dst_ref=target,
                send_sem=send_sem.at[phase, index],
                recv_sem=recv_sem.at[phase, index],
                device_id=place[side],
                device_id_type=MESH,
            ),
        )

    def stress_strike():
        return [
            remote(0, 0, "up", stress.at[1:3, 16:18], stress.at[1:3, 0:2]),
            remote(0, 1, "up", stress.at[0:1, 17:18], stress.at[0:1, 1:2]),
            remote(0, 2, "down", stress.at[1:3, 2:3], stress.at[1:3, 18:19]),
            remote(0, 3, "down", stress.at[0:1, 2:4], stress.at[0:1, 18:20]),
        ]

    def velocity_strike():
        return [
            remote(1, 0, "up", velocity.at[0:1, 16:18], velocity.at[0:1, 0:2]),
            remote(1, 1, "up", velocity.at[1:3, 17:18], velocity.at[1:3, 1:2]),
            remote(1, 2, "down", velocity.at[0:1, 2:3], velocity.at[0:1, 18:19]),
            remote(1, 3, "down", velocity.at[1:3, 2:4], velocity.at[1:3, 18:20]),
        ]

    def stress_cross(run):
        first, count = RUNS[run]
        own, halo = pl.ds(2 + first, count), pl.ds(first, count)
        base = 4 + 4 * run
        return [
            remote(
                0, base, "right", stress.at[2:4, own, 14:16], stress_halo.at[0:2, halo, 14:16]
            ),
            remote(
                0, base + 1, "right", stress.at[4:5, own, 15:16], stress_halo.at[2:3, halo, 15:16]
            ),
            remote(
                0, base + 2, "left", stress.at[2:4, own, 0:1], stress_halo.at[0:2, halo, 0:1]
            ),
            remote(
                0, base + 3, "left", stress.at[4:5, own, 0:2], stress_halo.at[2:3, halo, 0:2]
            ),
        ]

    def velocity_cross(run):
        first, count = RUNS[run]
        own, halo = pl.ds(2 + first, count), pl.ds(first, count)
        base = 4 + 4 * run
        return [
            remote(
                1, base, "right", velocity.at[2:3, own, 14:16], velocity_halo.at[2:3, halo, 14:16]
            ),
            remote(
                1,
                base + 1,
                "right",
                velocity.at[0:2, own, 15:16],
                velocity_halo.at[0:2, halo, 15:16],
            ),
            remote(
                1, base + 2, "left", velocity.at[2:3, own, 0:1], velocity_halo.at[2:3, halo, 0:1]
            ),
            remote(
                1, base + 3, "left", velocity.at[0:2, own, 0:2], velocity_halo.at[0:2, halo, 0:2]
            ),
        ]

    def start(copies):
        for side, copy in copies:

            @pl.when(has[side])
            def _(copy=copy):
                copy.start()

    def wait_recv(copies):
        for side, copy in copies:

            @pl.when(has[opposite[side]])
            def _(copy=copy):
                copy.wait_recv()

    def wait_send(copies):
        for side, copy in copies:

            @pl.when(has[side])
            def _(copy=copy):
                copy.wait_send()

    for copy in loads[:6]:
        copy.wait()
    start(stress_strike() + stress_cross(0) + stress_cross(1) + stress_cross(2))

    def pack_copy(step):
        other = lax.rem(cross + step, n_cross)
        return pltpu.make_async_remote_copy(
            src_ref=packed.at[cross],
            dst_ref=packed.at[cross],
            send_sem=pack_send.at[step],
            recv_sem=pack_recv.at[step],
            device_id=(strike, other),
            device_id_type=MESH,
        )

    for step in range(1, 8):
        pack_copy(step).start()

    for copy in loads[6:]:
        copy.wait()

    row = lax.broadcasted_iota(jnp.int32, (CY, NZ), 0)
    lane = lax.broadcasted_iota(jnp.int32, (CY, NZ), 1)

    def depth(value, offset):
        moved = pltpu.roll(value, (-offset) % NZ, 1)
        if offset < 0:
            return jnp.where(lane < -offset, 0.0, moved)
        return jnp.where(lane >= NZ - offset, 0.0, moved)

    def across(value, halo, offset):
        if offset < 0:
            joined = jnp.where(row >= CY + offset, halo, value)
        else:
            joined = jnp.where(row < offset, halo, value)
        return pltpu.roll(joined, (-offset) % CY, 0)

    def forward_depth(value):
        return (
            depth(value, 1) - value,
            depth(value, 2) - depth(value, -1),
        )

    def backward_depth(value):
        return (
            value - depth(value, -1),
            depth(value, 1) - depth(value, -2),
        )

    def forward_across(value, halo):
        return (
            across(value, halo, 1) - value,
            across(value, halo, 2) - across(value, halo, -1),
        )

    def backward_across(value, halo):
        return (
            value - across(value, halo, -1),
            across(value, halo, 1) - across(value, halo, -2),
        )

    def forward_strike(ref, comp, slab):
        return (
            ref[comp, slab + 1] - ref[comp, slab],
            ref[comp, slab + 2] - ref[comp, slab - 1],
        )

    def backward_strike(ref, comp, slab):
        return (
            ref[comp, slab] - ref[comp, slab - 1],
            ref[comp, slab + 1] - ref[comp, slab - 2],
        )

    def combine(*pairs):
        near, far = pairs[0]
        for pair in pairs[1:]:
            near, far = near + pair[0], far + pair[1]
        return NEAR * near - FAR * far

    def velocity_slab(x):
        slab = x + 2
        b = buoyancy[x]
        xy, yz, yy = stress[XY, slab], stress[YZ, slab], stress[YY, slab]
        xz, zz = stress[XZ, slab], stress[ZZ, slab]
        velocity[VX, slab] += b * combine(
            forward_strike(stress, XX, slab),
            backward_across(xy, stress_halo[0, x]),
            backward_depth(xz),
        )
        velocity[VY, slab] += b * combine(
            backward_strike(stress, XY, slab),
            forward_across(yy, stress_halo[2, x]),
            backward_depth(yz),
        )
        velocity[VZ, slab] += b * combine(
            backward_strike(stress, XZ, slab),
            backward_across(yz, stress_halo[1, x]),
            forward_depth(zz),
        )

    def stress_slab(x, r):
        slab = x + 2
        mu, la = shear[x], lame[x]
        vx, vy, vz = velocity[VX, slab], velocity[VY, slab], velocity[VZ, slab]
        hx, hz, hy = velocity_halo[0, x], velocity_halo[1, x], velocity_halo[2, x]
        ex = combine(backward_strike(velocity, VX, slab))
        ey = combine(backward_across(vy, hy))
        ez = combine(backward_depth(vz))
        spread = la * (ex + ey + ez)
        twice = 2.0 * mu
        stress[XX, slab] += spread + twice * ex
        stress[YY, slab] += spread + twice * ey
        stress[ZZ, slab] += spread + twice * ez
        sheared = stress[XY, slab] + mu * combine(
            forward_across(vx, hx), forward_strike(velocity, VY, slab)
        )
        stress[XY, slab] = sheared
        trial[pl.ds(r, 1), :] = sheared[0:1]
        stress[XZ, slab] += mu * combine(
            forward_depth(vx), forward_strike(velocity, VZ, slab)
        )
        stress[YZ, slab] += mu * combine(forward_depth(vy), forward_across(vz, hz))

    def outer(i):
        return i + jnp.where(i >= 4, 8, 0)

    def velocity_outer(i, carry):
        velocity_slab(outer(i))
        return carry

    def velocity_inner(i, carry):
        velocity_slab(i + 4)
        return carry

    def stress_outer(i, carry):
        stress_slab(outer(i), i)
        return carry

    def stress_inner(i, carry):
        stress_slab(i + 4, i + 8)
        return carry

    owner = fault_tile[strike]
    is_owner = owner == cross
    strike_of = (0, 1, 2, 3, 12, 13, 14, 15, 4, 5, 6, 7, 8, 9, 10, 11)

    for r, x in enumerate(strike_of):
        fault[0, r : r + 1, :] = shear[x, 0:1, :]
        ratio[r : r + 1, :] = buoyancy[x, 0:1, :]
    fault[0] = 0.5 * jnp.sqrt(fault[0] / ratio[...])

    def unpack():
        for step in range(1, 8):
            pack_copy(step).wait_recv()
        part = lax.broadcasted_iota(jnp.int32, (CX, 128), 1) // 32
        for half in range(2):
            blocks = [packed[4 * half + j] for j in range(4)]
            for index in range(4):
                value = None
                for j in range(4):
                    amount = (32 * (j - index)) % 128
                    moved = pltpu.roll(blocks[j], amount, 1) if amount else blocks[j]
                    value = moved if value is None else jnp.where(part == j, moved, value)
                fault[1 + index, :, 128 * half : 128 * half + 128] = value

    def friction(half):
        rows = slice(8 * half, 8 * half + 8)
        damping, before = fault[0, rows], fault[1, rows]
        a, psi = fault[3, rows], fault[4, rows]
        start_value = trial[rows]
        total = start_value + before
        width = 2.0 * ref_rate * jnp.exp(-psi / a)
        strength = a * fault[2, rows]
        scale = damping * width
        argument = total / scale
        magnitude = jnp.abs(argument)
        log = jnp.log(magnitude + jnp.sqrt(magnitude * magnitude + 1.0))
        u = jnp.where(argument < 0.0, -log, log)
        half_scale = 0.5 * scale
        for _ in range(NEWTON):
            grow, shrink = half_scale * jnp.exp(u), half_scale * jnp.exp(-u)
            u = u - (strength * u + (grow - shrink) - total) / (strength + (grow + shrink))
        slip = width * (0.5 * (jnp.exp(u) - jnp.exp(-u)))
        change = total - damping * slip - before
        fault[4, rows] = psi + evolve_rate * (
            jnp.exp((base_friction - psi) / evolve_b) - jnp.abs(slip) / ref_rate
        )
        fault[5, rows] = slip
        update = jnp.where(is_owner, change, start_value)
        for i in range(8):
            stress[XY, 2 + strike_of[8 * half + i], 0:1, :] = update[i : i + 1]

    def step_body(step, carry):
        wait_recv(stress_strike() + stress_cross(0) + stress_cross(1))

        @pl.when(step > 0)
        def _():
            wait_send(velocity_strike() + velocity_cross(0) + velocity_cross(1))

        lax.fori_loop(0, 8, velocity_outer, 0)
        start(velocity_strike() + velocity_cross(0) + velocity_cross(1))
        wait_recv(stress_cross(2))

        @pl.when(step > 0)
        def _():
            wait_send(velocity_cross(2))

        lax.fori_loop(0, 8, velocity_inner, 0)
        start(velocity_cross(2))

        @pl.when(step == 0)
        def _():
            unpack()

        wait_recv(velocity_strike() + velocity_cross(0) + velocity_cross(1))
        wait_send(stress_strike() + stress_cross(0) + stress_cross(1))
        lax.fori_loop(0, 8, stress_outer, 0)
        friction(0)

        @pl.when(step < STEPS - 1)
        def _():
            start(stress_strike() + stress_cross(0) + stress_cross(1))

        wait_recv(velocity_cross(2))
        wait_send(stress_cross(2))
        lax.fori_loop(0, 8, stress_inner, 0)
        friction(1)

        @pl.when(step < STEPS - 1)
        def _():
            start(stress_cross(2))

        return carry

    lax.fori_loop(0, STEPS, step_body, 0)
    wait_send(velocity_strike() + velocity_cross(0) + velocity_cross(1) + velocity_cross(2))

    for half in range(2):
        for j in range(4):
            lanes = slice(128 * half, 128 * half + 128)
            slip_part, state_part = fault[5, :, lanes], fault[4, :, lanes]
            first = pltpu.roll(slip_part, (128 - 32 * j) % 128, 1) if j else slip_part
            second = pltpu.roll(state_part, (160 - 32 * j) % 128, 1) if j != 1 else state_part
            part = lax.broadcasted_iota(jnp.int32, (CX, 128), 1)
            result[0, 4 * half + j] = jnp.where(part < 32, first, second)

    def result_copy(step):
        other = lax.rem(cross + step, n_cross)
        return pltpu.make_async_remote_copy(
            src_ref=result.at[0, other],
            dst_ref=result.at[1, cross],
            send_sem=result_send.at[step],
            recv_sem=result_recv.at[step],
            device_id=(strike, other),
            device_id_type=MESH,
        )

    for step in range(1, 8):
        result_copy(step).start()
    result[1, cross] = result[0, cross]

    stores = []
    for index, comp in enumerate(STRESS_ORDER):
        stores.append((stress.at[index, pl.ds(2, CX)], stress_out.at[comp]))
    for index, comp in enumerate(VELOCITY_ORDER):
        stores.append((velocity.at[index, pl.ds(2, CX)], velocity_out.at[comp]))
    stores = [
        pltpu.make_async_copy(source, target, store_sem.at[index])
        for index, (source, target) in enumerate(stores)
    ]
    for copy in stores:
        copy.start()
    for step in range(1, 8):
        result_copy(step).wait_recv()
    block = result[1, owner]
    for ref, first in ((slip_out, 0), (state_out, 32)):
        value = block[:, first : first + 32]
        ref[0:4] = value[0:4]
        ref[12:16] = value[4:8]
        ref[4:12] = value[8:16]
    for step in range(1, 8):
        pack_copy(step).wait_send()
        result_copy(step).wait_send()
    for copy in stores:
        copy.wait()


def write_kernel(a, b, c, d, a_out, b_out, c_out, d_out, sem):
    copies = [
        pltpu.make_async_copy(source, target, sem.at[index])
        for index, (source, target) in enumerate(((a, a_out), (b, b_out), (c, c_out), (d, d_out)))
    ]
    for copy in copies:
        copy.start()
    for copy in copies:
        copy.wait()


def local(
    velocity, stress, buoyancy, lame, shear, fault_tile, prestress, normal_stress, rate_a, state
):
    anywhere = pl.BlockSpec(memory_space=pl.ANY)
    vmem = pl.BlockSpec(memory_space=pltpu.VMEM)
    smem = pl.BlockSpec(memory_space=pltpu.SMEM)
    f32 = jnp.float32
    results = pl.pallas_call(
        wave_kernel,
        out_shape=(
            jax.ShapeDtypeStruct(velocity.shape, f32),
            jax.ShapeDtypeStruct(stress.shape, f32),
            jax.ShapeDtypeStruct(state.shape, f32),
            jax.ShapeDtypeStruct(state.shape, f32),
        ),
        in_specs=[anywhere] * 5 + [smem] + [vmem] * 4,
        out_specs=(anywhere, anywhere, vmem, vmem),
        scratch_shapes=[
            pltpu.VMEM((6, CX + 4, CY, NZ), f32),
            pltpu.VMEM((3, CX + 4, CY, NZ), f32),
            pltpu.VMEM((3, CX, CY, NZ), f32),
            pltpu.VMEM((3, CX, CY, NZ), f32),
            pltpu.VMEM((CX, CY, NZ), f32),
            pltpu.VMEM((CX, CY, NZ), f32),
            pltpu.VMEM((CX, CY, NZ), f32),
            pltpu.VMEM((CX, NZ), f32),
            pltpu.VMEM((CX, NZ), f32),
            pltpu.VMEM((6, CX, NZ), f32),
            pltpu.VMEM((8, CX, 128), f32),
            pltpu.VMEM((2, 8, CX, 128), f32),
            pltpu.SemaphoreType.DMA((2, 16)),
            pltpu.SemaphoreType.DMA((2, 16)),
            pltpu.SemaphoreType.DMA((8,)),
            pltpu.SemaphoreType.DMA((8,)),
            pltpu.SemaphoreType.DMA((8,)),
            pltpu.SemaphoreType.DMA((8,)),
            pltpu.SemaphoreType.DMA((12,)),
            pltpu.SemaphoreType.DMA((9,)),
        ],
        compiler_params=pltpu.CompilerParams(
            collective_id=0, has_side_effects=True, vmem_limit_bytes=48 * 2**20
        ),
    )(
        *[
            pltpu.with_memory_space_constraint(value, pltpu.HBM)
            for value in (
                stress,
                velocity,
                buoyancy,
                lame,
                shear,
                fault_tile,
                prestress,
                normal_stress,
                rate_a,
                state,
            )
        ]
    )
    return pl.pallas_call(
        write_kernel,
        out_shape=tuple(jax.ShapeDtypeStruct(value.shape, f32) for value in results),
        in_specs=[vmem] * 4,
        out_specs=(anywhere,) * 4,
        scratch_shapes=[pltpu.SemaphoreType.DMA((4,))],
    )(*[pltpu.with_memory_space_constraint(value, pltpu.VMEM) for value in results])


def solution(mesh):
    in_specs = (
        P(None, "strike", "cross", None),
        P(None, "strike", "cross", None),
        P("strike", "cross", None),
        P("strike", "cross", None),
        P("strike", "cross", None),
        P(),
        P("strike", "cross"),
        P("strike", "cross"),
        P("strike", "cross"),
        P("strike", "cross"),
    )
    out_specs = (
        P(None, "strike", "cross", None),
        P(None, "strike", "cross", None),
        P("strike", "cross"),
        P("strike", "cross"),
    )
    return jax.shard_map(local, mesh=mesh, in_specs=in_specs, out_specs=out_specs, check_vma=False)
```

```python
import jax
import jax.numpy as jnp
from jax import lax
from jax.experimental import pallas as pl
from jax.experimental.pallas import tpu as pltpu
from jax.sharding import PartitionSpec as P

STEPS = 4
NEWTON = 8

step_ratio = 0.25
ref_rate = 0.001
evolve_rate = 1e-05
base_friction = 0.6
evolve_b = 0.03

UNROLL = 3
CX = 16
CY = 16
NZ = 256
MESH = pl.DeviceIdType.MESH

XX, XZ, XY, YZ, YY, ZZ = range(6)
STRESS_ORDER = (0, 4, 3, 5, 1, 2)
VX, VZ, VY = range(3)
VELOCITY_ORDER = (0, 2, 1)

NEAR = step_ratio * 1.125
FAR = step_ratio / 24.0

INNER_RUNS = ((2, 6), (8, 6))
RUNS = ((0, 2), (14, 2)) + INNER_RUNS
COPIES = 6 + 4 * len(RUNS)

EDGE_ROWS = tuple(zip((0, 1, 2, 3), (0, 1, 14, 15)))
BASES = []
FAULT_ROWS = 8
for _first, _count in INNER_RUNS:
    BASES.append(FAULT_ROWS)
    FAULT_ROWS += -(-_count // 8) * 8
INNER_ROWS = tuple(
    tuple((base + i, first + i) for i in range(count))
    for base, (first, count) in zip(BASES, INNER_RUNS)
)


def wave_kernel(
    stress_in,
    velocity_in,
    buoyancy_in,
    lame_in,
    shear_in,
    fault_tile,
    prestress,
    normal_stress,
    rate_a,
    state,
    velocity_out,
    stress_out,
    slip_out,
    state_out,
    stress,
    velocity,
    stress_halo,
    velocity_halo,
    buoyancy,
    lame,
    shear,
    trial,
    ratio,
    fault,
    ordered,
    packed,
    result,
    send_sem,
    recv_sem,
    pack_send,
    pack_recv,
    result_send,
    result_recv,
    load_sem,
    store_sem,
):
    strike = lax.axis_index("strike")
    cross = lax.axis_index("cross")
    n_strike = lax.axis_size("strike")
    n_cross = lax.axis_size("cross")
    has = {
        "up": strike + 1 < n_strike,
        "down": strike >= 1,
        "right": cross + 1 < n_cross,
        "left": cross >= 1,
    }
    place = {
        "up": (strike + 1, cross),
        "down": (strike - 1, cross),
        "right": (strike, cross + 1),
        "left": (strike, cross - 1),
    }
    opposite = {"up": "down", "down": "up", "right": "left", "left": "right"}

    loads = []
    for index, comp in enumerate(STRESS_ORDER):
        loads.append((stress_in.at[comp], stress.at[index, pl.ds(2, CX)]))
    loads.append((buoyancy_in, buoyancy))
    for index, comp in enumerate(VELOCITY_ORDER):
        loads.append((velocity_in.at[comp], velocity.at[index, pl.ds(2, CX)]))
    loads.append((lame_in, lame))
    loads.append((shear_in, shear))
    loads = [
        pltpu.make_async_copy(source, target, load_sem.at[index])
        for index, (source, target) in enumerate(loads)
    ]
    for copy in loads:
        copy.start()

    zero_slab = jnp.zeros((CY, NZ), jnp.float32)
    for index in range(3):
        for slab in (0, 1, 18, 19):
            stress[index, slab] = zero_slab
            velocity[index, slab] = zero_slab

    def clear(slab, carry):
        for index in range(3):
            stress_halo[index, slab] = zero_slab
            velocity_halo[index, slab] = zero_slab
        return carry

    lax.fori_loop(0, CX, clear, 0)

    for index, ref in enumerate((prestress, normal_stress, rate_a, state)):
        packed[cross, :, pl.ds(32 * index, 32)] = ref[...]

    barrier = pltpu.get_barrier_semaphore()
    for side in ("up", "down"):

        @pl.when(has[side])
        def _(side=side):
            pl.semaphore_signal(barrier, inc=1, device_id=place[side], device_id_type=MESH)

    for step in range(1, 8):
        other = lax.rem(cross + step, n_cross)
        pl.semaphore_signal(barrier, inc=1, device_id=(strike, other), device_id_type=MESH)
    pl.semaphore_wait(
        barrier, 7 + has["up"].astype(jnp.int32) + has["down"].astype(jnp.int32)
    )

    def remote(phase, index, side, source, target):
        return (
            side,
            pltpu.make_async_remote_copy(
                src_ref=source,
                dst_ref=target,
                send_sem=send_sem.at[phase, index],
                recv_sem=recv_sem.at[phase, index],
                device_id=place[side],
                device_id_type=MESH,
            ),
        )

    def stress_strike():
        return [
            remote(0, 0, "up", stress.at[XZ, 16:18], stress.at[XZ, 0:2]),
            remote(0, 1, "up", stress.at[XX, 17:18], stress.at[XX, 1:2]),
            remote(0, 2, "down", stress.at[XZ, 2:3], stress.at[XZ, 18:19]),
            remote(0, 3, "down", stress.at[XX, 2:4], stress.at[XX, 18:20]),
            remote(0, 4, "up", stress.at[XY, 16:18], stress.at[XY, 0:2]),
            remote(0, 5, "down", stress.at[XY, 2:3], stress.at[XY, 18:19]),
        ]

    def velocity_strike():
        return [
            remote(1, 0, "up", velocity.at[0:1, 16:18], velocity.at[0:1, 0:2]),
            remote(1, 1, "up", velocity.at[1:3, 17:18], velocity.at[1:3, 1:2]),
            remote(1, 2, "down", velocity.at[0:1, 2:3], velocity.at[0:1, 18:19]),
            remote(1, 3, "down", velocity.at[1:3, 2:4], velocity.at[1:3, 18:20]),
        ]

    def stress_cross(run):
        first, count = RUNS[run]
        own, halo = pl.ds(2 + first, count), pl.ds(first, count)
        base = 6 + 4 * run
        return [
            remote(
                0, base, "right", stress.at[2:4, own, 14:16], stress_halo.at[0:2, halo, 14:16]
            ),
            remote(
                0, base + 1, "right", stress.at[4:5, own, 15:16], stress_halo.at[2:3, halo, 15:16]
            ),
            remote(
                0, base + 2, "left", stress.at[2:4, own, 0:1], stress_halo.at[0:2, halo, 0:1]
            ),
            remote(
                0, base + 3, "left", stress.at[4:5, own, 0:2], stress_halo.at[2:3, halo, 0:2]
            ),
        ]

    def velocity_cross(run):
        first, count = RUNS[run]
        own, halo = pl.ds(2 + first, count), pl.ds(first, count)
        base = 6 + 4 * run
        return [
            remote(
                1, base, "right", velocity.at[2:3, own, 14:16], velocity_halo.at[2:3, halo, 14:16]
            ),
            remote(
                1,
                base + 1,
                "right",
                velocity.at[0:2, own, 15:16],
                velocity_halo.at[0:2, halo, 15:16],
            ),
            remote(
                1, base + 2, "left", velocity.at[2:3, own, 0:1], velocity_halo.at[2:3, halo, 0:1]
            ),
            remote(
                1, base + 3, "left", velocity.at[0:2, own, 0:2], velocity_halo.at[0:2, halo, 0:2]
            ),
        ]

    def start(copies):
        for side, copy in copies:

            @pl.when(has[side])
            def _(copy=copy):
                copy.start()

    def wait_recv(copies):
        for side, copy in copies:

            @pl.when(has[opposite[side]])
            def _(copy=copy):
                copy.wait_recv()

    def wait_send(copies):
        for side, copy in copies:

            @pl.when(has[side])
            def _(copy=copy):
                copy.wait_send()

    for copy in loads[:6]:
        copy.wait()
    start(stress_strike() + stress_cross(0) + stress_cross(1))
    wait_send(stress_strike() + stress_cross(0) + stress_cross(1))
    start([c for run in range(2, len(RUNS)) for c in stress_cross(run)])

    def pack_copy(step):
        other = lax.rem(cross + step, n_cross)
        return pltpu.make_async_remote_copy(
            src_ref=packed.at[cross],
            dst_ref=packed.at[cross],
            send_sem=pack_send.at[step],
            recv_sem=pack_recv.at[step],
            device_id=(strike, other),
            device_id_type=MESH,
        )

    for step in range(1, 8):
        pack_copy(step).start()

    for copy in loads[6:]:
        copy.wait()

    row = lax.broadcasted_iota(jnp.int32, (8, 128), 0)
    lane = lax.broadcasted_iota(jnp.int32, (8, 128), 1)
    nothing = jnp.zeros((8, 128), jnp.float32)

    def tile(ref, index, slab, a, b):
        return ref[index, slab, 8 * a : 8 * a + 8, 128 * b : 128 * b + 128]

    def tiles(ref, index, slab):
        return [[tile(ref, index, slab, a, b) for b in range(2)] for a in range(2)]

    def move(here, beside, offset, axis, size):
        place = row if axis == 0 else lane
        if offset < 0:
            joined = jnp.where(place >= size + offset, beside, here)
        else:
            joined = jnp.where(place < offset, beside, here)
        return pltpu.roll(joined, (-offset) % size, axis)

    def depth(field, a, b, offset):
        other = b + (1 if offset > 0 else -1)
        beside = field[a][other] if 0 <= other < 2 else nothing
        return move(field[a][b], beside, offset, 1, 128)

    def across(field, a, b, offset):
        other = a + (1 if offset > 0 else -1)
        beside = field[other][b] if 0 <= other < 2 else field[2][other % 2][b]
        return move(field[a][b], beside, offset, 0, 8)

    def forward(shift, field, a, b):
        here = field[a][b]
        return (
            shift(field, a, b, 1) - here,
            shift(field, a, b, 2) - shift(field, a, b, -1),
        )

    def backward(shift, field, a, b):
        here = field[a][b]
        return (
            here - shift(field, a, b, -1),
            shift(field, a, b, 1) - shift(field, a, b, -2),
        )

    def forward_strike(ref, index, slab, here, a, b):
        return (
            tile(ref, index, slab + 1, a, b) - here,
            tile(ref, index, slab + 2, a, b) - tile(ref, index, slab - 1, a, b),
        )

    def backward_strike(ref, index, slab, here, a, b):
        return (
            here - tile(ref, index, slab - 1, a, b),
            tile(ref, index, slab + 1, a, b) - tile(ref, index, slab - 2, a, b),
        )

    def combine(*pairs):
        near, far = pairs[0]
        for pair in pairs[1:]:
            near, far = near + pair[0], far + pair[1]
        return near - (FAR / NEAR) * far

    def velocity_slab(x):
        slab = x + 2
        xx, yy, zz = (tiles(stress, index, slab) for index in (XX, YY, ZZ))
        xy, xz, yz = (tiles(stress, index, slab) for index in (XY, XZ, YZ))
        xy.append(tiles(stress_halo, 0, x))
        yz.append(tiles(stress_halo, 1, x))
        yy.append(tiles(stress_halo, 2, x))
        results = []
        for a in range(2):
            for b in range(2):
                factor = NEAR * buoyancy[x, 8 * a : 8 * a + 8, 128 * b : 128 * b + 128]
                rate_x = combine(
                    forward_strike(stress, XX, slab, xx[a][b], a, b),
                    backward(across, xy, a, b),
                    backward(depth, xz, a, b),
                )
                rate_y = combine(
                    backward_strike(stress, XY, slab, xy[a][b], a, b),
                    forward(across, yy, a, b),
                    backward(depth, yz, a, b),
                )
                rate_z = combine(
                    backward_strike(stress, XZ, slab, xz[a][b], a, b),
                    backward(across, yz, a, b),
                    forward(depth, zz, a, b),
                )
                for index, rate in ((VX, rate_x), (VY, rate_y), (VZ, rate_z)):
                    results.append((index, a, b, tile(velocity, index, slab, a, b) + factor * rate))
        for index, a, b, value in results:
            velocity[index, slab, 8 * a : 8 * a + 8, 128 * b : 128 * b + 128] = value

    def stress_slab(x, r):
        slab = x + 2
        vx, vy, vz = (tiles(velocity, index, slab) for index in (VX, VY, VZ))
        vx.append(tiles(velocity_halo, 0, x))
        vz.append(tiles(velocity_halo, 1, x))
        vy.append(tiles(velocity_halo, 2, x))
        results = []
        for a in range(2):
            for b in range(2):
                mu = NEAR * shear[x, 8 * a : 8 * a + 8, 128 * b : 128 * b + 128]
                la = NEAR * lame[x, 8 * a : 8 * a + 8, 128 * b : 128 * b + 128]
                ex = combine(backward_strike(velocity, VX, slab, vx[a][b], a, b))
                ey = combine(backward(across, vy, a, b))
                ez = combine(backward(depth, vz, a, b))
                spread = la * (ex + ey + ez)
                twice = mu + mu
                changes = (
                    (XX, spread + twice * ex),
                    (YY, spread + twice * ey),
                    (ZZ, spread + twice * ez),
                    (
                        XY,
                        mu
                        * combine(
                            forward(across, vx, a, b),
                            forward_strike(velocity, VY, slab, vy[a][b], a, b),
                        ),
                    ),
                    (
                        XZ,
                        mu
                        * combine(
                            forward(depth, vx, a, b),
                            forward_strike(velocity, VZ, slab, vz[a][b], a, b),
                        ),
                    ),
                    (YZ, mu * combine(forward(depth, vy, a, b), forward(across, vz, a, b))),
                )
                for index, change in changes:
                    results.append((index, a, b, tile(stress, index, slab, a, b) + change))
        for index, a, b, value in results:
            stress[index, slab, 8 * a : 8 * a + 8, 128 * b : 128 * b + 128] = value
        first = [value[0:1] for index, a, b, value in results if index == XY and a == 0]
        trial[pl.ds(r, 1), :] = jnp.concatenate(first, axis=1)

    def outer(i):
        return i + jnp.where(i >= 2, 12, 0)

    def velocity_outer(i, carry):
        velocity_slab(outer(i))
        return carry

    def stress_outer(i, carry):
        stress_slab(outer(i), i)
        return carry

    def velocity_inner(run):
        first, count = INNER_RUNS[run]

        def body(i, carry):
            velocity_slab(i + first)
            return carry

        lax.fori_loop(0, count, body, 0, unroll=UNROLL)

    def stress_inner(run):
        first, count = INNER_RUNS[run]

        def body(i, carry):
            stress_slab(i + first, i + BASES[run])
            return carry

        lax.fori_loop(0, count, body, 0, unroll=UNROLL)

    owner = fault_tile[strike]
    is_owner = owner == cross

    for r, x in EDGE_ROWS + sum(INNER_ROWS, ()):
        fault[0, r : r + 1, :] = shear[x, 0:1, :]
        ratio[r : r + 1, :] = buoyancy[x, 0:1, :]
    for cells in (EDGE_ROWS,) + INNER_ROWS:
        rows = slice(cells[0][0], cells[-1][0] + 1)
        fault[0, rows] = 0.5 * jnp.sqrt(fault[0, rows] / ratio[rows])

    def unpack():
        for step in range(1, 8):
            pack_copy(step).wait_recv()
        part = lax.broadcasted_iota(jnp.int32, (CX, 128), 1) // 32
        for half in range(2):
            blocks = [packed[4 * half + j] for j in range(4)]
            for index in range(4):
                value = None
                for j in range(4):
                    amount = (32 * (j - index)) % 128
                    moved = pltpu.roll(blocks[j], amount, 1) if amount else blocks[j]
                    value = moved if value is None else jnp.where(part == j, moved, value)
                lanes = slice(128 * half, 128 * half + 128)
                fault[1 + index, 0:2, lanes] = value[0:2]
                fault[1 + index, 2:4, lanes] = value[14:16]
                for base, (first, count) in zip(BASES, INNER_RUNS):
                    fault[1 + index, base : base + count, lanes] = value[first : first + count]

    def friction(cells):
        first = cells[0][0]
        rows = slice(first, first + len(cells))
        damping, before = fault[0, rows], fault[1, rows]
        a, psi = fault[3, rows], fault[4, rows]
        start_value = trial[rows]
        total = start_value + before
        width = 2.0 * ref_rate * jnp.exp(-psi / a)
        strength = a * fault[2, rows]
        scale = damping * width
        argument = total / scale
        magnitude = jnp.abs(argument)
        log = jnp.log(magnitude + jnp.sqrt(magnitude * magnitude + 1.0))
        u = jnp.where(argument < 0.0, -log, log)
        half_scale = 0.5 * scale
        for _ in range(NEWTON):
            grow, shrink = half_scale * jnp.exp(u), half_scale * jnp.exp(-u)
            u = u - (strength * u + (grow - shrink) - total) / (strength + (grow + shrink))
        slip = width * (0.5 * (jnp.exp(u) - jnp.exp(-u)))
        change = total - damping * slip - before
        fault[4, rows] = psi + evolve_rate * (
            jnp.exp((base_friction - psi) / evolve_b) - jnp.abs(slip) / ref_rate
        )
        fault[5, rows] = slip
        update = jnp.where(is_owner, change, start_value)
        for r, x in cells:
            stress[XY, 2 + x, 0:1, :] = update[r - first : r - first + 1]

    def split(along, over):
        free, tied = along[:4], along[4:]
        for index, copy in enumerate(over):
            (tied if index % 4 == 2 else free).append(copy)
        return free, tied

    def step_body(step, carry):
        wait_recv(stress_strike() + stress_cross(0) + stress_cross(1))

        lax.fori_loop(0, 4, velocity_outer, 0, unroll=2)
        start(velocity_strike() + velocity_cross(0) + velocity_cross(1))
        for run in range(len(INNER_RUNS)):
            wait_recv(stress_cross(2 + run))

            @pl.when(step > 0)
            def _(run=run):
                wait_send(velocity_cross(2 + run))

            velocity_inner(run)
            if run == 0:
                wait_send(velocity_strike() + velocity_cross(0) + velocity_cross(1))
            start(velocity_cross(2 + run))

        @pl.when(step == 0)
        def _():
            unpack()

        wait_recv(velocity_strike() + velocity_cross(0) + velocity_cross(1))
        lax.fori_loop(0, 4, stress_outer, 0, unroll=2)
        free, tied = split(stress_strike(), stress_cross(0) + stress_cross(1))

        @pl.when(step < STEPS - 1)
        def _():
            start(free)

        friction(EDGE_ROWS)

        @pl.when(step < STEPS - 1)
        def _():
            start(tied)

        for run in range(len(INNER_RUNS)):
            wait_recv(velocity_cross(2 + run))
            wait_send(stress_cross(2 + run))
            stress_inner(run)
            free, tied = split([], stress_cross(2 + run))

            @pl.when(step < STEPS - 1)
            def _(free=free, run=run):
                if run == 0:
                    wait_send(stress_strike() + stress_cross(0) + stress_cross(1))
                start(free)

            friction(INNER_ROWS[run])

            @pl.when(step < STEPS - 1)
            def _(tied=tied):
                start(tied)

        return carry

    lax.fori_loop(0, STEPS, step_body, 0)
    wait_send([c for run in range(2, len(RUNS)) for c in velocity_cross(run)])

    for index, which in enumerate((5, 4)):
        ordered[index, 0:2] = fault[which, 0:2]
        ordered[index, 14:16] = fault[which, 2:4]
        for base, (first, count) in zip(BASES, INNER_RUNS):
            ordered[index, first : first + count] = fault[which, base : base + count]
    for half in range(2):
        for j in range(4):
            lanes = slice(128 * half, 128 * half + 128)
            slip_part, state_part = ordered[0, :, lanes], ordered[1, :, lanes]
            first = pltpu.roll(slip_part, (128 - 32 * j) % 128, 1) if j else slip_part
            second = pltpu.roll(state_part, (160 - 32 * j) % 128, 1) if j != 1 else state_part
            part = lax.broadcasted_iota(jnp.int32, (CX, 128), 1)
            result[0, 4 * half + j] = jnp.where(part < 32, first, second)

    def result_copy(step):
        other = lax.rem(cross + step, n_cross)
        return pltpu.make_async_remote_copy(
            src_ref=result.at[0, other],
            dst_ref=result.at[1, cross],
            send_sem=result_send.at[step],
            recv_sem=result_recv.at[step],
            device_id=(strike, other),
            device_id_type=MESH,
        )

    for step in range(1, 8):
        result_copy(step).start()
    result[1, cross] = result[0, cross]

    stores = []
    for index, comp in enumerate(STRESS_ORDER):
        stores.append((stress.at[index, pl.ds(2, CX)], stress_out.at[comp]))
    for index, comp in enumerate(VELOCITY_ORDER):
        stores.append((velocity.at[index, pl.ds(2, CX)], velocity_out.at[comp]))
    stores = [
        pltpu.make_async_copy(source, target, store_sem.at[index])
        for index, (source, target) in enumerate(stores)
    ]
    for copy in stores:
        copy.start()
    for step in range(1, 8):
        result_copy(step).wait_recv()
    block = result[1, owner]
    for ref, first in ((slip_out, 0), (state_out, 32)):
        ref[...] = block[:, first : first + 32]
    for step in range(1, 8):
        pack_copy(step).wait_send()
        result_copy(step).wait_send()
    for copy in stores:
        copy.wait()


def write_kernel(a, b, c, d, a_out, b_out, c_out, d_out, sem):
    copies = [
        pltpu.make_async_copy(source, target, sem.at[index])
        for index, (source, target) in enumerate(((a, a_out), (b, b_out), (c, c_out), (d, d_out)))
    ]
    for copy in copies:
        copy.start()
    for copy in copies:
        copy.wait()


def local(
    velocity, stress, buoyancy, lame, shear, fault_tile, prestress, normal_stress, rate_a, state
):
    anywhere = pl.BlockSpec(memory_space=pl.ANY)
    vmem = pl.BlockSpec(memory_space=pltpu.VMEM)
    smem = pl.BlockSpec(memory_space=pltpu.SMEM)
    f32 = jnp.float32
    results = pl.pallas_call(
        wave_kernel,
        out_shape=(
            jax.ShapeDtypeStruct(velocity.shape, f32),
            jax.ShapeDtypeStruct(stress.shape, f32),
            jax.ShapeDtypeStruct(state.shape, f32),
            jax.ShapeDtypeStruct(state.shape, f32),
        ),
        in_specs=[anywhere] * 5 + [smem] + [vmem] * 4,
        out_specs=(anywhere, anywhere, vmem, vmem),
        scratch_shapes=[
            pltpu.VMEM((6, CX + 4, CY, NZ), f32),
            pltpu.VMEM((3, CX + 4, CY, NZ), f32),
            pltpu.VMEM((3, CX, CY, NZ), f32),
            pltpu.VMEM((3, CX, CY, NZ), f32),
            pltpu.VMEM((CX, CY, NZ), f32),
            pltpu.VMEM((CX, CY, NZ), f32),
            pltpu.VMEM((CX, CY, NZ), f32),
            pltpu.VMEM((FAULT_ROWS, NZ), f32),
            pltpu.VMEM((FAULT_ROWS, NZ), f32),
            pltpu.VMEM((6, FAULT_ROWS, NZ), f32),
            pltpu.VMEM((2, CX, NZ), f32),
            pltpu.VMEM((8, CX, 128), f32),
            pltpu.VMEM((2, 8, CX, 128), f32),
            pltpu.SemaphoreType.DMA((2, COPIES)),
            pltpu.SemaphoreType.DMA((2, COPIES)),
            pltpu.SemaphoreType.DMA((8,)),
            pltpu.SemaphoreType.DMA((8,)),
            pltpu.SemaphoreType.DMA((8,)),
            pltpu.SemaphoreType.DMA((8,)),
            pltpu.SemaphoreType.DMA((12,)),
            pltpu.SemaphoreType.DMA((9,)),
        ],
        compiler_params=pltpu.CompilerParams(
            collective_id=0, has_side_effects=True, vmem_limit_bytes=48 * 2**20
        ),
    )(
        *[
            pltpu.with_memory_space_constraint(value, pltpu.HBM)
            for value in (
                stress,
                velocity,
                buoyancy,
                lame,
                shear,
                fault_tile,
                prestress,
                normal_stress,
                rate_a,
                state,
            )
        ]
    )
    return pl.pallas_call(
        write_kernel,
        out_shape=tuple(jax.ShapeDtypeStruct(value.shape, f32) for value in results),
        in_specs=[vmem] * 4,
        out_specs=(anywhere,) * 4,
        scratch_shapes=[pltpu.SemaphoreType.DMA((4,))],
    )(*[pltpu.with_memory_space_constraint(value, pltpu.VMEM) for value in results])


def solution(mesh):
    in_specs = (
        P(None, "strike", "cross", None),
        P(None, "strike", "cross", None),
        P("strike", "cross", None),
        P("strike", "cross", None),
        P("strike", "cross", None),
        P(),
        P("strike", "cross"),
        P("strike", "cross"),
        P("strike", "cross"),
        P("strike", "cross"),
    )
    out_specs = (
        P(None, "strike", "cross", None),
        P(None, "strike", "cross", None),
        P("strike", "cross"),
        P("strike", "cross"),
    )
    return jax.shard_map(local, mesh=mesh, in_specs=in_specs, out_specs=out_specs, check_vma=False)
```

```python
import jax
import jax.numpy as jnp
from jax import lax
from jax.experimental import pallas as pl
from jax.experimental.pallas import tpu as pltpu
from jax.sharding import PartitionSpec as P

STEPS = 4
NEWTON = 8

step_ratio = 0.25
ref_rate = 0.001
evolve_rate = 1e-05
base_friction = 0.6
evolve_b = 0.03

CX = 16
CY = 16
NZ = 256
MESH = pl.DeviceIdType.MESH

XX, XZ, XY, YZ, YY, ZZ = range(6)
STRESS_ORDER = (0, 4, 3, 5, 1, 2)
VX, VZ, VY = range(3)
VELOCITY_ORDER = (0, 2, 1)

NEAR = step_ratio * 1.125
FAR = step_ratio / 24.0

RUNS = ((2, 0, 14), (8, 8, 0), (6, 2, 8))
UNROLLS = (2, 2, 3)
COPIES = 6 + 4 * len(RUNS)
BASES = (0, 8, 16)
FAULT_ROWS = 24


def wave_kernel(
    stress_in,
    velocity_in,
    buoyancy_in,
    lame_in,
    shear_in,
    fault_tile,
    prestress,
    normal_stress,
    rate_a,
    state,
    velocity_out,
    stress_out,
    slip_out,
    state_out,
    stress,
    velocity,
    stress_halo,
    velocity_halo,
    buoyancy,
    lame,
    shear,
    trial,
    ratio,
    fault,
    ordered,
    packed,
    result,
    send_sem,
    recv_sem,
    pack_send,
    pack_recv,
    result_send,
    result_recv,
    load_sem,
    store_sem,
):
    strike = lax.axis_index("strike")
    cross = lax.axis_index("cross")
    n_strike = lax.axis_size("strike")
    n_cross = lax.axis_size("cross")
    odd = lax.rem(strike, 2)
    is_odd = odd == 1
    first_of = [even + (late - even) * odd for _, even, late in RUNS]
    has = {
        "up": strike + 1 < n_strike,
        "down": strike >= 1,
        "right": cross + 1 < n_cross,
        "left": cross >= 1,
    }
    place = {
        "up": (strike + 1, cross),
        "down": (strike - 1, cross),
        "right": (strike, cross + 1),
        "left": (strike, cross - 1),
    }
    opposite = {"up": "down", "down": "up", "right": "left", "left": "right"}

    loads = []
    for index, comp in enumerate(STRESS_ORDER):
        loads.append((stress_in.at[comp], stress.at[index, pl.ds(2, CX)]))
    loads.append((buoyancy_in, buoyancy))
    for index, comp in enumerate(VELOCITY_ORDER):
        loads.append((velocity_in.at[comp], velocity.at[index, pl.ds(2, CX)]))
    loads.append((lame_in, lame))
    loads.append((shear_in, shear))
    loads = [
        pltpu.make_async_copy(source, target, load_sem.at[index])
        for index, (source, target) in enumerate(loads)
    ]
    for copy in loads:
        copy.start()

    zero_slab = jnp.zeros((CY, NZ), jnp.float32)
    for index in range(3):
        for slab in (0, 1, 18, 19):
            stress[index, slab] = zero_slab
            velocity[index, slab] = zero_slab

    def clear(slab, carry):
        for index in range(3):
            stress_halo[index, slab] = zero_slab
            velocity_halo[index, slab] = zero_slab
        return carry

    lax.fori_loop(0, CX, clear, 0)

    for index, ref in enumerate((prestress, normal_stress, rate_a, state)):
        packed[cross, :, pl.ds(32 * index, 32)] = ref[...]

    barrier = pltpu.get_barrier_semaphore()
    for side in ("up", "down"):

        @pl.when(has[side])
        def _(side=side):
            pl.semaphore_signal(barrier, inc=1, device_id=place[side], device_id_type=MESH)

    for step in range(1, 8):
        other = lax.rem(cross + step, n_cross)
        pl.semaphore_signal(barrier, inc=1, device_id=(strike, other), device_id_type=MESH)
    pl.semaphore_wait(
        barrier, 7 + has["up"].astype(jnp.int32) + has["down"].astype(jnp.int32)
    )

    def remote(phase, index, side, source, target):
        return (
            side,
            pltpu.make_async_remote_copy(
                src_ref=source,
                dst_ref=target,
                send_sem=send_sem.at[phase, index],
                recv_sem=recv_sem.at[phase, index],
                device_id=place[side],
                device_id_type=MESH,
            ),
        )

    def stress_strike():
        return [
            remote(0, 0, "up", stress.at[XZ, 16:18], stress.at[XZ, 0:2]),
            remote(0, 1, "up", stress.at[XX, 17:18], stress.at[XX, 1:2]),
            remote(0, 2, "down", stress.at[XZ, 2:3], stress.at[XZ, 18:19]),
            remote(0, 3, "down", stress.at[XX, 2:4], stress.at[XX, 18:20]),
            remote(0, 4, "up", stress.at[XY, 16:18], stress.at[XY, 0:2]),
            remote(0, 5, "down", stress.at[XY, 2:3], stress.at[XY, 18:19]),
        ]

    def velocity_strike():
        return [
            remote(1, 0, "up", velocity.at[0:1, 16:18], velocity.at[0:1, 0:2]),
            remote(1, 1, "up", velocity.at[1:3, 17:18], velocity.at[1:3, 1:2]),
            remote(1, 2, "down", velocity.at[0:1, 2:3], velocity.at[0:1, 18:19]),
            remote(1, 3, "down", velocity.at[1:3, 2:4], velocity.at[1:3, 18:20]),
        ]

    def stress_cross(run):
        first, count = first_of[run], RUNS[run][0]
        own, halo = pl.ds(2 + first, count), pl.ds(first, count)
        base = 6 + 4 * run
        return [
            remote(
                0, base, "right", stress.at[2:4, own, 14:16], stress_halo.at[0:2, halo, 14:16]
            ),
            remote(
                0, base + 1, "right", stress.at[4:5, own, 15:16], stress_halo.at[2:3, halo, 15:16]
            ),
            remote(
                0, base + 2, "left", stress.at[2:4, own, 0:1], stress_halo.at[0:2, halo, 0:1]
            ),
            remote(
                0, base + 3, "left", stress.at[4:5, own, 0:2], stress_halo.at[2:3, halo, 0:2]
            ),
        ]

    def velocity_cross(run):
        first, count = first_of[run], RUNS[run][0]
        own, halo = pl.ds(2 + first, count), pl.ds(first, count)
        base = 6 + 4 * run
        return [
            remote(
                1, base, "right", velocity.at[2:3, own, 14:16], velocity_halo.at[2:3, halo, 14:16]
            ),
            remote(
                1,
                base + 1,
                "right",
                velocity.at[0:2, own, 15:16],
                velocity_halo.at[0:2, halo, 15:16],
            ),
            remote(
                1, base + 2, "left", velocity.at[2:3, own, 0:1], velocity_halo.at[2:3, halo, 0:1]
            ),
            remote(
                1, base + 3, "left", velocity.at[0:2, own, 0:2], velocity_halo.at[0:2, halo, 0:2]
            ),
        ]

    def start(copies, far=None):
        for side, copy in copies:

            @pl.when(sending(side, far))
            def _(copy=copy):
                copy.start()

    def wait_recv(copies, far=None):
        for side, copy in copies:

            @pl.when(receiving(side, far))
            def _(copy=copy):
                copy.wait_recv()

    def wait_send(copies, far=None):
        for side, copy in copies:

            @pl.when(sending(side, far))
            def _(copy=copy):
                copy.wait_send()

    def sending(side, far):
        if far is None:
            return has[side]
        return jnp.logical_and(has[side], is_odd if far == (side == "up") else odd == 0)

    def receiving(side, far):
        if far is None:
            return has[opposite[side]]
        return jnp.logical_and(
            has[opposite[side]], is_odd if far == (side == "down") else odd == 0
        )

    for copy in loads[:6]:
        copy.wait()
    start(stress_strike() + stress_cross(0) + stress_cross(1) + stress_cross(2))
    wait_send(stress_strike(), True)
    wait_send(stress_cross(0))

    def pack_copy(step):
        other = lax.rem(cross + step, n_cross)
        return pltpu.make_async_remote_copy(
            src_ref=packed.at[cross],
            dst_ref=packed.at[cross],
            send_sem=pack_send.at[step],
            recv_sem=pack_recv.at[step],
            device_id=(strike, other),
            device_id_type=MESH,
        )

    for step in range(1, 8):
        pack_copy(step).start()

    for copy in loads[6:]:
        copy.wait()

    row = lax.broadcasted_iota(jnp.int32, (8, 128), 0)
    lane = lax.broadcasted_iota(jnp.int32, (8, 128), 1)
    nothing = jnp.zeros((8, 128), jnp.float32)

    def tile(ref, index, slab, a, b):
        return ref[index, slab, 8 * a : 8 * a + 8, 128 * b : 128 * b + 128]

    def tiles(ref, index, slab):
        return [[tile(ref, index, slab, a, b) for b in range(2)] for a in range(2)]

    def move(here, beside, offset, axis, size):
        place = row if axis == 0 else lane
        if offset < 0:
            joined = jnp.where(place >= size + offset, beside, here)
        else:
            joined = jnp.where(place < offset, beside, here)
        return pltpu.roll(joined, (-offset) % size, axis)

    def depth(field, a, b, offset):
        other = b + (1 if offset > 0 else -1)
        beside = field[a][other] if 0 <= other < 2 else nothing
        return move(field[a][b], beside, offset, 1, 128)

    def across(field, a, b, offset):
        other = a + (1 if offset > 0 else -1)
        beside = field[other][b] if 0 <= other < 2 else field[2][other % 2][b]
        return move(field[a][b], beside, offset, 0, 8)

    def forward(shift, field, a, b):
        here = field[a][b]
        return (
            shift(field, a, b, 1) - here,
            shift(field, a, b, 2) - shift(field, a, b, -1),
        )

    def backward(shift, field, a, b):
        here = field[a][b]
        return (
            here - shift(field, a, b, -1),
            shift(field, a, b, 1) - shift(field, a, b, -2),
        )

    def forward_strike(ref, index, slab, here, a, b):
        return (
            tile(ref, index, slab + 1, a, b) - here,
            tile(ref, index, slab + 2, a, b) - tile(ref, index, slab - 1, a, b),
        )

    def backward_strike(ref, index, slab, here, a, b):
        return (
            here - tile(ref, index, slab - 1, a, b),
            tile(ref, index, slab + 1, a, b) - tile(ref, index, slab - 2, a, b),
        )

    def combine(*pairs):
        near, far = pairs[0]
        for pair in pairs[1:]:
            near, far = near + pair[0], far + pair[1]
        return near - (FAR / NEAR) * far

    def velocity_slab(x):
        slab = x + 2
        xx, yy, zz = (tiles(stress, index, slab) for index in (XX, YY, ZZ))
        xy, xz, yz = (tiles(stress, index, slab) for index in (XY, XZ, YZ))
        xy.append(tiles(stress_halo, 0, x))
        yz.append(tiles(stress_halo, 1, x))
        yy.append(tiles(stress_halo, 2, x))
        results = []
        for a in range(2):
            for b in range(2):
                factor = NEAR * buoyancy[x, 8 * a : 8 * a + 8, 128 * b : 128 * b + 128]
                rate_x = combine(
                    forward_strike(stress, XX, slab, xx[a][b], a, b),
                    backward(across, xy, a, b),
                    backward(depth, xz, a, b),
                )
                rate_y = combine(
                    backward_strike(stress, XY, slab, xy[a][b], a, b),
                    forward(across, yy, a, b),
                    backward(depth, yz, a, b),
                )
                rate_z = combine(
                    backward_strike(stress, XZ, slab, xz[a][b], a, b),
                    backward(across, yz, a, b),
                    forward(depth, zz, a, b),
                )
                for index, rate in ((VX, rate_x), (VY, rate_y), (VZ, rate_z)):
                    results.append((index, a, b, tile(velocity, index, slab, a, b) + factor * rate))
        for index, a, b, value in results:
            velocity[index, slab, 8 * a : 8 * a + 8, 128 * b : 128 * b + 128] = value

    def stress_slab(x, r):
        slab = x + 2
        vx, vy, vz = (tiles(velocity, index, slab) for index in (VX, VY, VZ))
        vx.append(tiles(velocity_halo, 0, x))
        vz.append(tiles(velocity_halo, 1, x))
        vy.append(tiles(velocity_halo, 2, x))
        results = []
        for a in range(2):
            for b in range(2):
                mu = NEAR * shear[x, 8 * a : 8 * a + 8, 128 * b : 128 * b + 128]
                la = NEAR * lame[x, 8 * a : 8 * a + 8, 128 * b : 128 * b + 128]
                ex = combine(backward_strike(velocity, VX, slab, vx[a][b], a, b))
                ey = combine(backward(across, vy, a, b))
                ez = combine(backward(depth, vz, a, b))
                spread = la * (ex + ey + ez)
                twice = mu + mu
                changes = (
                    (XX, spread + twice * ex),
                    (YY, spread + twice * ey),
                    (ZZ, spread + twice * ez),
                    (
                        XY,
                        mu
                        * combine(
                            forward(across, vx, a, b),
                            forward_strike(velocity, VY, slab, vy[a][b], a, b),
                        ),
                    ),
                    (
                        XZ,
                        mu
                        * combine(
                            forward(depth, vx, a, b),
                            forward_strike(velocity, VZ, slab, vz[a][b], a, b),
                        ),
                    ),
                    (YZ, mu * combine(forward(depth, vy, a, b), forward(across, vz, a, b))),
                )
                for index, change in changes:
                    results.append((index, a, b, tile(stress, index, slab, a, b) + change))
        for index, a, b, value in results:
            stress[index, slab, 8 * a : 8 * a + 8, 128 * b : 128 * b + 128] = value
        first = [value[0:1] for index, a, b, value in results if index == XY and a == 0]
        trial[pl.ds(r, 1), :] = jnp.concatenate(first, axis=1)

    def velocity_run(run):
        def body(i, carry):
            velocity_slab(i + first_of[run])
            return carry

        lax.fori_loop(0, RUNS[run][0], body, 0, unroll=UNROLLS[run])

    def stress_run(run):
        def body(i, carry):
            stress_slab(i + first_of[run], i + BASES[run])
            return carry

        lax.fori_loop(0, RUNS[run][0], body, 0, unroll=UNROLLS[run])

    owner = fault_tile[strike]
    is_owner = owner == cross

    for run, base in enumerate(BASES):
        rows = slice(base, base + RUNS[run][0])
        for i in range(RUNS[run][0]):
            fault[0, base + i : base + i + 1, :] = shear[first_of[run] + i, 0:1, :]
            ratio[base + i : base + i + 1, :] = buoyancy[first_of[run] + i, 0:1, :]
        fault[0, rows] = 0.5 * jnp.sqrt(fault[0, rows] / ratio[rows])

    def unpack():
        for step in range(1, 8):
            pack_copy(step).wait_recv()
        part = lax.broadcasted_iota(jnp.int32, (CX, 128), 1) // 32
        for half in range(2):
            blocks = [packed[4 * half + j] for j in range(4)]
            for index in range(4):
                value = None
                for j in range(4):
                    amount = (32 * (j - index)) % 128
                    moved = pltpu.roll(blocks[j], amount, 1) if amount else blocks[j]
                    value = moved if value is None else jnp.where(part == j, moved, value)
                lanes = slice(128 * half, 128 * half + 128)
                for base, (count, even, late) in zip(BASES, RUNS):
                    fault[1 + index, base : base + count, lanes] = jnp.where(
                        is_odd, value[late : late + count], value[even : even + count]
                    )

    def friction(run):
        count = RUNS[run][0]
        rows = slice(BASES[run], BASES[run] + count)
        damping, before = fault[0, rows], fault[1, rows]
        a, psi = fault[3, rows], fault[4, rows]
        start_value = trial[rows]
        total = start_value + before
        width = 2.0 * ref_rate * jnp.exp(-psi / a)
        strength = a * fault[2, rows]
        scale = damping * width
        argument = total / scale
        magnitude = jnp.abs(argument)
        log = jnp.log(magnitude + jnp.sqrt(magnitude * magnitude + 1.0))
        u = jnp.where(argument < 0.0, -log, log)
        half_scale = 0.5 * scale
        for _ in range(NEWTON):
            grow, shrink = half_scale * jnp.exp(u), half_scale * jnp.exp(-u)
            u = u - (strength * u + (grow - shrink) - total) / (strength + (grow + shrink))
        slip = width * (0.5 * (jnp.exp(u) - jnp.exp(-u)))
        change = total - damping * slip - before
        fault[4, rows] = psi + evolve_rate * (
            jnp.exp((base_friction - psi) / evolve_b) - jnp.abs(slip) / ref_rate
        )
        fault[5, rows] = slip
        update = jnp.where(is_owner, change, start_value)
        for i in range(count):
            stress[XY, 2 + first_of[run] + i, 0:1, :] = update[i : i + 1]

    def split(copies):
        return copies[:2] + copies[3:], copies[2:3]

    def step_body(step, carry):
        for run in range(3):
            if run < 2:
                wait_recv(stress_strike(), run == 0)
            wait_recv(stress_cross(run))
            if run > 0:

                @pl.when(step > 0)
                def _(run=run):
                    if run == 1:
                        wait_send(velocity_strike(), False)
                    wait_send(velocity_cross(run))

            velocity_run(run)
            if run < 2:
                start(velocity_strike(), run == 0)
            start(velocity_cross(run))
            if run == 2:
                wait_send(velocity_strike(), True)
                wait_send(velocity_cross(0))

        @pl.when(step == 0)
        def _():
            unpack()

        for run in range(3):
            if run < 2:
                wait_recv(velocity_strike(), run == 0)
            wait_recv(velocity_cross(run))
            if run > 0:
                if run == 1:
                    wait_send(stress_strike(), False)
                wait_send(stress_cross(run))
            stress_run(run)
            free, tied = split(stress_cross(run))
            along = stress_strike()

            @pl.when(step < STEPS - 1)
            def _(run=run, free=free, along=along):
                if run < 2:
                    start(along[:4], run == 0)
                start(free)
                if run == 2:
                    wait_send(along, True)
                    wait_send(stress_cross(0))

            friction(run)

            @pl.when(step < STEPS - 1)
            def _(run=run, tied=tied, along=along):
                if run < 2:
                    start(along[4:], run == 0)
                start(tied)

        return carry

    lax.fori_loop(0, STEPS, step_body, 0)
    wait_send(velocity_strike(), False)
    wait_send(velocity_cross(1) + velocity_cross(2))

    for index, which in enumerate((5, 4)):
        for base, (count, even, late) in zip(BASES, RUNS):
            value = fault[which, base : base + count]
            ordered[index, even : even + count] = value
            ordered[2 + index, late : late + count] = value
        ordered[index] = jnp.where(is_odd, ordered[2 + index], ordered[index])
    for half in range(2):
        for j in range(4):
            lanes = slice(128 * half, 128 * half + 128)
            slip_part, state_part = ordered[0, :, lanes], ordered[1, :, lanes]
            first = pltpu.roll(slip_part, (128 - 32 * j) % 128, 1) if j else slip_part
            second = pltpu.roll(state_part, (160 - 32 * j) % 128, 1) if j != 1 else state_part
            part = lax.broadcasted_iota(jnp.int32, (CX, 128), 1)
            result[0, 4 * half + j] = jnp.where(part < 32, first, second)

    def result_copy(step):
        other = lax.rem(cross + step, n_cross)
        return pltpu.make_async_remote_copy(
            src_ref=result.at[0, other],
            dst_ref=result.at[1, cross],
            send_sem=result_send.at[step],
            recv_sem=result_recv.at[step],
            device_id=(strike, other),
            device_id_type=MESH,
        )

    for step in range(1, 8):
        result_copy(step).start()
    result[1, cross] = result[0, cross]

    stores = []
    for index, comp in enumerate(STRESS_ORDER):
        stores.append((stress.at[index, pl.ds(2, CX)], stress_out.at[comp]))
    for index, comp in enumerate(VELOCITY_ORDER):
        stores.append((velocity.at[index, pl.ds(2, CX)], velocity_out.at[comp]))
    stores = [
        pltpu.make_async_copy(source, target, store_sem.at[index])
        for index, (source, target) in enumerate(stores)
    ]
    for copy in stores:
        copy.start()
    for step in range(1, 8):
        result_copy(step).wait_recv()
    block = result[1, owner]
    for ref, first in ((slip_out, 0), (state_out, 32)):
        ref[...] = block[:, first : first + 32]
    for step in range(1, 8):
        pack_copy(step).wait_send()
        result_copy(step).wait_send()
    for copy in stores:
        copy.wait()


def write_kernel(a, b, c, d, a_out, b_out, c_out, d_out, sem):
    copies = [
        pltpu.make_async_copy(source, target, sem.at[index])
        for index, (source, target) in enumerate(((a, a_out), (b, b_out), (c, c_out), (d, d_out)))
    ]
    for copy in copies:
        copy.start()
    for copy in copies:
        copy.wait()


def local(
    velocity, stress, buoyancy, lame, shear, fault_tile, prestress, normal_stress, rate_a, state
):
    anywhere = pl.BlockSpec(memory_space=pl.ANY)
    vmem = pl.BlockSpec(memory_space=pltpu.VMEM)
    smem = pl.BlockSpec(memory_space=pltpu.SMEM)
    f32 = jnp.float32
    results = pl.pallas_call(
        wave_kernel,
        out_shape=(
            jax.ShapeDtypeStruct(velocity.shape, f32),
            jax.ShapeDtypeStruct(stress.shape, f32),
            jax.ShapeDtypeStruct(state.shape, f32),
            jax.ShapeDtypeStruct(state.shape, f32),
        ),
        in_specs=[anywhere] * 5 + [smem] + [vmem] * 4,
        out_specs=(anywhere, anywhere, vmem, vmem),
        scratch_shapes=[
            pltpu.VMEM((6, CX + 4, CY, NZ), f32),
            pltpu.VMEM((3, CX + 4, CY, NZ), f32),
            pltpu.VMEM((3, CX, CY, NZ), f32),
            pltpu.VMEM((3, CX, CY, NZ), f32),
            pltpu.VMEM((CX, CY, NZ), f32),
            pltpu.VMEM((CX, CY, NZ), f32),
            pltpu.VMEM((CX, CY, NZ), f32),
            pltpu.VMEM((FAULT_ROWS, NZ), f32),
            pltpu.VMEM((FAULT_ROWS, NZ), f32),
            pltpu.VMEM((6, FAULT_ROWS, NZ), f32),
            pltpu.VMEM((4, CX, NZ), f32),
            pltpu.VMEM((8, CX, 128), f32),
            pltpu.VMEM((2, 8, CX, 128), f32),
            pltpu.SemaphoreType.DMA((2, COPIES)),
            pltpu.SemaphoreType.DMA((2, COPIES)),
            pltpu.SemaphoreType.DMA((8,)),
            pltpu.SemaphoreType.DMA((8,)),
            pltpu.SemaphoreType.DMA((8,)),
            pltpu.SemaphoreType.DMA((8,)),
            pltpu.SemaphoreType.DMA((12,)),
            pltpu.SemaphoreType.DMA((9,)),
        ],
        compiler_params=pltpu.CompilerParams(
            collective_id=0, has_side_effects=True, vmem_limit_bytes=48 * 2**20
        ),
    )(
        *[
            pltpu.with_memory_space_constraint(value, pltpu.HBM)
            for value in (
                stress,
                velocity,
                buoyancy,
                lame,
                shear,
                fault_tile,
                prestress,
                normal_stress,
                rate_a,
                state,
            )
        ]
    )
    return pl.pallas_call(
        write_kernel,
        out_shape=tuple(jax.ShapeDtypeStruct(value.shape, f32) for value in results),
        in_specs=[vmem] * 4,
        out_specs=(anywhere,) * 4,
        scratch_shapes=[pltpu.SemaphoreType.DMA((4,))],
    )(*[pltpu.with_memory_space_constraint(value, pltpu.VMEM) for value in results])


def solution(mesh):
    in_specs = (
        P(None, "strike", "cross", None),
        P(None, "strike", "cross", None),
        P("strike", "cross", None),
        P("strike", "cross", None),
        P("strike", "cross", None),
        P(),
        P("strike", "cross"),
        P("strike", "cross"),
        P("strike", "cross"),
        P("strike", "cross"),
    )
    out_specs = (
        P(None, "strike", "cross", None),
        P(None, "strike", "cross", None),
        P("strike", "cross"),
        P("strike", "cross"),
    )
    return jax.shard_map(local, mesh=mesh, in_specs=in_specs, out_specs=out_specs, check_vma=False)
```

```python
import jax
import jax.numpy as jnp
from jax import lax
from jax.experimental import pallas as pl
from jax.experimental.pallas import tpu as pltpu
from jax.sharding import PartitionSpec as P

STEPS = 4
NEWTON = 8

step_ratio = 0.25
ref_rate = 0.001
evolve_rate = 1e-05
base_friction = 0.6
evolve_b = 0.03

CX = 16
CY = 16
NZ = 256
MESH = pl.DeviceIdType.MESH

XX, XZ, XY, YZ, YY, ZZ = range(6)
STRESS_ORDER = (0, 4, 3, 5, 1, 2)
VX, VZ, VY = range(3)
VELOCITY_ORDER = (0, 2, 1)

NEAR = step_ratio * 1.125
FAR = step_ratio / 24.0

RUNS = ((2, 0, 14), (8, 8, 0), (6, 2, 8))
UNROLLS = (2, 2, 3)
COPIES = 6 + 4 * len(RUNS)
BASES = (0, 8, 16)
FAULT_ROWS = 24


def wave_kernel(
    stress_in,
    velocity_in,
    buoyancy_in,
    lame_in,
    shear_in,
    fault_tile,
    prestress,
    normal_stress,
    rate_a,
    state,
    velocity_out,
    stress_out,
    slip_out,
    state_out,
    stress,
    velocity,
    stress_halo,
    velocity_halo,
    buoyancy,
    lame,
    shear,
    trial,
    ratio,
    fault,
    ordered,
    packed,
    result,
    send_sem,
    recv_sem,
    pack_send,
    pack_recv,
    result_send,
    result_recv,
    load_sem,
    store_sem,
):
    strike = lax.axis_index("strike")
    cross = lax.axis_index("cross")
    n_strike = lax.axis_size("strike")
    n_cross = lax.axis_size("cross")
    odd = lax.rem(strike, 2)
    is_odd = odd == 1
    first_of = [even + (late - even) * odd for _, even, late in RUNS]
    has = {
        "up": strike + 1 < n_strike,
        "down": strike >= 1,
        "right": cross + 1 < n_cross,
        "left": cross >= 1,
    }
    place = {
        "up": (strike + 1, cross),
        "down": (strike - 1, cross),
        "right": (strike, cross + 1),
        "left": (strike, cross - 1),
    }
    opposite = {"up": "down", "down": "up", "right": "left", "left": "right"}

    loads = []
    for index, comp in enumerate(STRESS_ORDER):
        loads.append((stress_in.at[comp], stress.at[index, pl.ds(2, CX)]))
    loads.append((buoyancy_in, buoyancy))
    for index, comp in enumerate(VELOCITY_ORDER):
        loads.append((velocity_in.at[comp], velocity.at[index, pl.ds(2, CX)]))
    loads.append((lame_in, lame))
    loads.append((shear_in, shear))
    loads = [
        pltpu.make_async_copy(source, target, load_sem.at[index])
        for index, (source, target) in enumerate(loads)
    ]
    for copy in loads:
        copy.start()

    zero_slab = jnp.zeros((CY, NZ), jnp.float32)
    for index in range(3):
        for slab in (0, 1, 18, 19):
            stress[index, slab] = zero_slab
            velocity[index, slab] = zero_slab

    def clear(slab, carry):
        for index in range(3):
            stress_halo[index, slab] = zero_slab
            velocity_halo[index, slab] = zero_slab
        return carry

    lax.fori_loop(0, CX, clear, 0)

    for index, ref in enumerate((prestress, normal_stress, rate_a, state)):
        packed[cross, :, pl.ds(32 * index, 32)] = ref[...]

    barrier = pltpu.get_barrier_semaphore()
    for side in ("up", "down"):

        @pl.when(has[side])
        def _(side=side):
            pl.semaphore_signal(barrier, inc=1, device_id=place[side], device_id_type=MESH)

    for step in range(1, 8):
        other = lax.rem(cross + step, n_cross)
        pl.semaphore_signal(barrier, inc=1, device_id=(strike, other), device_id_type=MESH)
    pl.semaphore_wait(
        barrier, 7 + has["up"].astype(jnp.int32) + has["down"].astype(jnp.int32)
    )

    def remote(phase, index, side, source, target):
        return (
            side,
            pltpu.make_async_remote_copy(
                src_ref=source,
                dst_ref=target,
                send_sem=send_sem.at[phase, index],
                recv_sem=recv_sem.at[phase, index],
                device_id=place[side],
                device_id_type=MESH,
            ),
        )

    def stress_strike():
        return [
            remote(0, 0, "up", stress.at[XZ, 16:18], stress.at[XZ, 0:2]),
            remote(0, 1, "up", stress.at[XX, 17:18], stress.at[XX, 1:2]),
            remote(0, 2, "down", stress.at[XZ, 2:3], stress.at[XZ, 18:19]),
            remote(0, 3, "down", stress.at[XX, 2:4], stress.at[XX, 18:20]),
            remote(0, 4, "up", stress.at[XY, 16:18], stress.at[XY, 0:2]),
            remote(0, 5, "down", stress.at[XY, 2:3], stress.at[XY, 18:19]),
        ]

    def velocity_strike():
        return [
            remote(1, 0, "up", velocity.at[0:1, 16:18], velocity.at[0:1, 0:2]),
            remote(1, 1, "up", velocity.at[1:3, 17:18], velocity.at[1:3, 1:2]),
            remote(1, 2, "down", velocity.at[0:1, 2:3], velocity.at[0:1, 18:19]),
            remote(1, 3, "down", velocity.at[1:3, 2:4], velocity.at[1:3, 18:20]),
        ]

    def stress_cross(run):
        first, count = first_of[run], RUNS[run][0]
        own, halo = pl.ds(2 + first, count), pl.ds(first, count)
        base = 6 + 4 * run
        return [
            remote(
                0, base, "right", stress.at[2:4, own, 14:16], stress_halo.at[0:2, halo, 14:16]
            ),
            remote(
                0, base + 1, "right", stress.at[4:5, own, 15:16], stress_halo.at[2:3, halo, 15:16]
            ),
            remote(
                0, base + 2, "left", stress.at[2:4, own, 0:1], stress_halo.at[0:2, halo, 0:1]
            ),
            remote(
                0, base + 3, "left", stress.at[4:5, own, 0:2], stress_halo.at[2:3, halo, 0:2]
            ),
        ]

    def velocity_cross(run):
        first, count = first_of[run], RUNS[run][0]
        own, halo = pl.ds(2 + first, count), pl.ds(first, count)
        base = 6 + 4 * run
        return [
            remote(
                1, base, "right", velocity.at[2:3, own, 14:16], velocity_halo.at[2:3, halo, 14:16]
            ),
            remote(
                1,
                base + 1,
                "right",
                velocity.at[0:2, own, 15:16],
                velocity_halo.at[0:2, halo, 15:16],
            ),
            remote(
                1, base + 2, "left", velocity.at[2:3, own, 0:1], velocity_halo.at[2:3, halo, 0:1]
            ),
            remote(
                1, base + 3, "left", velocity.at[0:2, own, 0:2], velocity_halo.at[0:2, halo, 0:2]
            ),
        ]

    def start(copies, far=None):
        for side, copy in copies:

            @pl.when(sending(side, far))
            def _(copy=copy):
                copy.start()

    def wait_recv(copies, far=None):
        for side, copy in copies:

            @pl.when(receiving(side, far))
            def _(copy=copy):
                copy.wait_recv()

    def wait_send(copies, far=None):
        for side, copy in copies:

            @pl.when(sending(side, far))
            def _(copy=copy):
                copy.wait_send()

    def sending(side, far):
        if far is None:
            return has[side]
        return jnp.logical_and(has[side], is_odd if far == (side == "up") else odd == 0)

    def receiving(side, far):
        if far is None:
            return has[opposite[side]]
        return jnp.logical_and(
            has[opposite[side]], is_odd if far == (side == "down") else odd == 0
        )

    for copy in loads[:6]:
        copy.wait()
    start(stress_strike() + stress_cross(0) + stress_cross(1) + stress_cross(2))
    wait_send(stress_strike(), True)
    wait_send(stress_cross(0))

    def pack_copy(step):
        other = lax.rem(cross + step, n_cross)
        return pltpu.make_async_remote_copy(
            src_ref=packed.at[cross],
            dst_ref=packed.at[cross],
            send_sem=pack_send.at[step],
            recv_sem=pack_recv.at[step],
            device_id=(strike, other),
            device_id_type=MESH,
        )

    for copy in loads[6:]:
        copy.wait()

    row = lax.broadcasted_iota(jnp.int32, (8, 128), 0)
    lane = lax.broadcasted_iota(jnp.int32, (8, 128), 1)
    nothing = jnp.zeros((8, 128), jnp.float32)

    def tile(ref, index, slab, a, b):
        return ref[index, slab, 8 * a : 8 * a + 8, 128 * b : 128 * b + 128]

    def tiles(ref, index, slab):
        return [[tile(ref, index, slab, a, b) for b in range(2)] for a in range(2)]

    def move(here, beside, offset, axis, size):
        place = row if axis == 0 else lane
        if offset < 0:
            joined = jnp.where(place >= size + offset, beside, here)
        else:
            joined = jnp.where(place < offset, beside, here)
        return pltpu.roll(joined, (-offset) % size, axis)

    def depth(field, a, b, offset):
        other = b + (1 if offset > 0 else -1)
        beside = field[a][other] if 0 <= other < 2 else nothing
        return move(field[a][b], beside, offset, 1, 128)

    def across(field, a, b, offset):
        other = a + (1 if offset > 0 else -1)
        beside = field[other][b] if 0 <= other < 2 else field[2][other % 2][b]
        return move(field[a][b], beside, offset, 0, 8)

    def forward(shift, field, a, b):
        here = field[a][b]
        return (
            shift(field, a, b, 1) - here,
            shift(field, a, b, 2) - shift(field, a, b, -1),
        )

    def backward(shift, field, a, b):
        here = field[a][b]
        return (
            here - shift(field, a, b, -1),
            shift(field, a, b, 1) - shift(field, a, b, -2),
        )

    def forward_strike(ref, index, slab, here, a, b):
        return (
            tile(ref, index, slab + 1, a, b) - here,
            tile(ref, index, slab + 2, a, b) - tile(ref, index, slab - 1, a, b),
        )

    def backward_strike(ref, index, slab, here, a, b):
        return (
            here - tile(ref, index, slab - 1, a, b),
            tile(ref, index, slab + 1, a, b) - tile(ref, index, slab - 2, a, b),
        )

    def combine(*pairs):
        near, far = pairs[0]
        for pair in pairs[1:]:
            near, far = near + pair[0], far + pair[1]
        return near - (FAR / NEAR) * far

    def velocity_slab(x):
        slab = x + 2
        xx, yy, zz = (tiles(stress, index, slab) for index in (XX, YY, ZZ))
        xy, xz, yz = (tiles(stress, index, slab) for index in (XY, XZ, YZ))
        xy.append(tiles(stress_halo, 0, x))
        yz.append(tiles(stress_halo, 1, x))
        yy.append(tiles(stress_halo, 2, x))
        results = []
        for a in range(2):
            for b in range(2):
                factor = NEAR * buoyancy[x, 8 * a : 8 * a + 8, 128 * b : 128 * b + 128]
                rate_x = combine(
                    forward_strike(stress, XX, slab, xx[a][b], a, b),
                    backward(across, xy, a, b),
                    backward(depth, xz, a, b),
                )
                rate_y = combine(
                    backward_strike(stress, XY, slab, xy[a][b], a, b),
                    forward(across, yy, a, b),
                    backward(depth, yz, a, b),
                )
                rate_z = combine(
                    backward_strike(stress, XZ, slab, xz[a][b], a, b),
                    backward(across, yz, a, b),
                    forward(depth, zz, a, b),
                )
                for index, rate in ((VX, rate_x), (VY, rate_y), (VZ, rate_z)):
                    results.append((index, a, b, tile(velocity, index, slab, a, b) + factor * rate))
        for index, a, b, value in results:
            velocity[index, slab, 8 * a : 8 * a + 8, 128 * b : 128 * b + 128] = value

    def stress_slab(x, r):
        slab = x + 2
        vx, vy, vz = (tiles(velocity, index, slab) for index in (VX, VY, VZ))
        vx.append(tiles(velocity_halo, 0, x))
        vz.append(tiles(velocity_halo, 1, x))
        vy.append(tiles(velocity_halo, 2, x))
        results = []
        for a in range(2):
            for b in range(2):
                mu = NEAR * shear[x, 8 * a : 8 * a + 8, 128 * b : 128 * b + 128]
                la = NEAR * lame[x, 8 * a : 8 * a + 8, 128 * b : 128 * b + 128]
                ex = combine(backward_strike(velocity, VX, slab, vx[a][b], a, b))
                ey = combine(backward(across, vy, a, b))
                ez = combine(backward(depth, vz, a, b))
                spread = la * (ex + ey + ez)
                twice = mu + mu
                changes = (
                    (XX, spread + twice * ex),
                    (YY, spread + twice * ey),
                    (ZZ, spread + twice * ez),
                    (
                        XY,
                        mu
                        * combine(
                            forward(across, vx, a, b),
                            forward_strike(velocity, VY, slab, vy[a][b], a, b),
                        ),
                    ),
                    (
                        XZ,
                        mu
                        * combine(
                            forward(depth, vx, a, b),
                            forward_strike(velocity, VZ, slab, vz[a][b], a, b),
                        ),
                    ),
                    (YZ, mu * combine(forward(depth, vy, a, b), forward(across, vz, a, b))),
                )
                for index, change in changes:
                    results.append((index, a, b, tile(stress, index, slab, a, b) + change))
        for index, a, b, value in results:
            stress[index, slab, 8 * a : 8 * a + 8, 128 * b : 128 * b + 128] = value
        first = [value[0:1] for index, a, b, value in results if index == XY and a == 0]
        trial[pl.ds(r, 1), :] = jnp.concatenate(first, axis=1)

    def velocity_run(run):
        def body(i, carry):
            velocity_slab(i + first_of[run])
            return carry

        lax.fori_loop(0, RUNS[run][0], body, 0, unroll=UNROLLS[run])

    def stress_run(run):
        def body(i, carry):
            stress_slab(i + first_of[run], i + BASES[run])
            return carry

        lax.fori_loop(0, RUNS[run][0], body, 0, unroll=UNROLLS[run])

    owner = fault_tile[strike]
    is_owner = owner == cross

    for run, base in enumerate(BASES):
        rows = slice(base, base + RUNS[run][0])
        for i in range(RUNS[run][0]):
            fault[0, base + i : base + i + 1, :] = shear[first_of[run] + i, 0:1, :]
            ratio[base + i : base + i + 1, :] = buoyancy[first_of[run] + i, 0:1, :]
        fault[0, rows] = 0.5 * jnp.sqrt(fault[0, rows] / ratio[rows])

    def unpack():
        for step in range(1, 8):
            pack_copy(step).wait_recv()
        part = lax.broadcasted_iota(jnp.int32, (CX, 128), 1) // 32
        for half in range(2):
            blocks = [packed[4 * half + j] for j in range(4)]
            for index in range(4):
                value = None
                for j in range(4):
                    amount = (32 * (j - index)) % 128
                    moved = pltpu.roll(blocks[j], amount, 1) if amount else blocks[j]
                    value = moved if value is None else jnp.where(part == j, moved, value)
                lanes = slice(128 * half, 128 * half + 128)
                for base, (count, even, late) in zip(BASES, RUNS):
                    fault[1 + index, base : base + count, lanes] = jnp.where(
                        is_odd, value[late : late + count], value[even : even + count]
                    )

    def friction(run):
        count = RUNS[run][0]
        rows = slice(BASES[run], BASES[run] + count)
        damping, before = fault[0, rows], fault[1, rows]
        a, psi = fault[3, rows], fault[4, rows]
        start_value = trial[rows]
        total = start_value + before
        width = 2.0 * ref_rate * jnp.exp(-psi / a)
        strength = a * fault[2, rows]
        scale = damping * width
        argument = total / scale
        magnitude = jnp.abs(argument)
        log = jnp.log(magnitude + jnp.sqrt(magnitude * magnitude + 1.0))
        u = jnp.where(argument < 0.0, -log, log)
        half_scale = 0.5 * scale
        for _ in range(NEWTON):
            grow, shrink = half_scale * jnp.exp(u), half_scale * jnp.exp(-u)
            u = u - (strength * u + (grow - shrink) - total) / (strength + (grow + shrink))
        slip = width * (0.5 * (jnp.exp(u) - jnp.exp(-u)))
        change = total - damping * slip - before
        fault[4, rows] = psi + evolve_rate * (
            jnp.exp((base_friction - psi) / evolve_b) - jnp.abs(slip) / ref_rate
        )
        fault[5, rows] = slip
        update = jnp.where(is_owner, change, start_value)
        for i in range(count):
            stress[XY, 2 + first_of[run] + i, 0:1, :] = update[i : i + 1]

    def split(copies):
        return copies[:2] + copies[3:], copies[2:3]

    def step_body(step, carry):
        for run in range(3):
            if run < 2:
                wait_recv(stress_strike(), run == 0)
            wait_recv(stress_cross(run))
            if run > 0:

                @pl.when(step > 0)
                def _(run=run):
                    if run == 1:
                        wait_send(velocity_strike(), False)
                    wait_send(velocity_cross(run))

            velocity_run(run)
            if run < 2:
                start(velocity_strike(), run == 0)
            start(velocity_cross(run))
            if run == 0:

                @pl.when(step == 0)
                def _():
                    for other in range(1, 8):
                        pack_copy(other).start()

            if run == 2:
                wait_send(velocity_strike(), True)
                wait_send(velocity_cross(0))

        for run in range(3):
            if run < 2:
                wait_recv(velocity_strike(), run == 0)
            wait_recv(velocity_cross(run))
            if run > 0:
                if run == 1:
                    wait_send(stress_strike(), False)
                wait_send(stress_cross(run))
            stress_run(run)
            free, tied = split(stress_cross(run))
            along = stress_strike()

            @pl.when(step < STEPS - 1)
            def _(run=run, free=free, along=along):
                if run < 2:
                    start(along[:4], run == 0)
                start(free)
                if run == 2:
                    wait_send(along, True)
                    wait_send(stress_cross(0))

            if run == 0:

                @pl.when(step == 0)
                def _():
                    unpack()

            friction(run)

            @pl.when(step < STEPS - 1)
            def _(run=run, tied=tied, along=along):
                if run < 2:
                    start(along[4:], run == 0)
                start(tied)

        return carry

    lax.fori_loop(0, STEPS, step_body, 0)
    wait_send(velocity_strike(), False)
    wait_send(velocity_cross(1) + velocity_cross(2))

    for index, which in enumerate((5, 4)):
        for base, (count, even, late) in zip(BASES, RUNS):
            value = fault[which, base : base + count]
            ordered[index, even : even + count] = value
            ordered[2 + index, late : late + count] = value
        ordered[index] = jnp.where(is_odd, ordered[2 + index], ordered[index])
    for half in range(2):
        for j in range(4):
            lanes = slice(128 * half, 128 * half + 128)
            part = lax.broadcasted_iota(jnp.int32, (8, 128), 1) // 32
            value = None
            for index in range(4):
                piece = ordered[index // 2, 8 * (index % 2) : 8 * (index % 2) + 8, lanes]
                amount = (32 * (index - j)) % 128
                moved = pltpu.roll(piece, amount, 1) if amount else piece
                value = moved if value is None else jnp.where(part == index, moved, value)
            result[0, 4 * half + j] = value

    def result_copy(step):
        other = lax.rem(cross + step, n_cross)
        return pltpu.make_async_remote_copy(
            src_ref=result.at[0, other],
            dst_ref=result.at[1, cross],
            send_sem=result_send.at[step],
            recv_sem=result_recv.at[step],
            device_id=(strike, other),
            device_id_type=MESH,
        )

    for step in range(1, 8):
        result_copy(step).start()
    result[1, cross] = result[0, cross]

    stores = []
    for index, comp in enumerate(STRESS_ORDER):
        stores.append((stress.at[index, pl.ds(2, CX)], stress_out.at[comp]))
    for index, comp in enumerate(VELOCITY_ORDER):
        stores.append((velocity.at[index, pl.ds(2, CX)], velocity_out.at[comp]))
    stores = [
        pltpu.make_async_copy(source, target, store_sem.at[index])
        for index, (source, target) in enumerate(stores)
    ]
    for copy in stores:
        copy.start()
    for step in range(1, 8):
        result_copy(step).wait_recv()
    block = result[1, owner]
    for ref, first in ((slip_out, 0), (state_out, 64)):
        ref[0:8] = block[:, first : first + 32]
        ref[8:16] = block[:, first + 32 : first + 64]
    for step in range(1, 8):
        pack_copy(step).wait_send()
        result_copy(step).wait_send()
    for copy in stores:
        copy.wait()


def write_kernel(a, b, c, d, a_out, b_out, c_out, d_out, sem):
    pairs = [(b.at[index], b_out.at[index]) for index in range(6)]
    pairs += [(a.at[index], a_out.at[index]) for index in range(3)]
    pairs += [(c, c_out), (d, d_out)]
    copies = [
        pltpu.make_async_copy(source, target, sem.at[index])
        for index, (source, target) in enumerate(pairs)
    ]
    for copy in copies:
        copy.start()
    for copy in copies:
        copy.wait()


def local(
    velocity, stress, buoyancy, lame, shear, fault_tile, prestress, normal_stress, rate_a, state
):
    anywhere = pl.BlockSpec(memory_space=pl.ANY)
    vmem = pl.BlockSpec(memory_space=pltpu.VMEM)
    smem = pl.BlockSpec(memory_space=pltpu.SMEM)
    f32 = jnp.float32
    results = pl.pallas_call(
        wave_kernel,
        out_shape=(
            jax.ShapeDtypeStruct(velocity.shape, f32),
            jax.ShapeDtypeStruct(stress.shape, f32),
            jax.ShapeDtypeStruct(state.shape, f32),
            jax.ShapeDtypeStruct(state.shape, f32),
        ),
        in_specs=[anywhere] * 5 + [smem] + [vmem] * 4,
        out_specs=(anywhere, anywhere, vmem, vmem),
        scratch_shapes=[
            pltpu.VMEM((6, CX + 4, CY, NZ), f32),
            pltpu.VMEM((3, CX + 4, CY, NZ), f32),
            pltpu.VMEM((3, CX, CY, NZ), f32),
            pltpu.VMEM((3, CX, CY, NZ), f32),
            pltpu.VMEM((CX, CY, NZ), f32),
            pltpu.VMEM((CX, CY, NZ), f32),
            pltpu.VMEM((CX, CY, NZ), f32),
            pltpu.VMEM((FAULT_ROWS, NZ), f32),
            pltpu.VMEM((FAULT_ROWS, NZ), f32),
            pltpu.VMEM((6, FAULT_ROWS, NZ), f32),
            pltpu.VMEM((4, CX, NZ), f32),
            pltpu.VMEM((8, CX, 128), f32),
            pltpu.VMEM((2, 8, 8, 128), f32),
            pltpu.SemaphoreType.DMA((2, COPIES)),
            pltpu.SemaphoreType.DMA((2, COPIES)),
            pltpu.SemaphoreType.DMA((8,)),
            pltpu.SemaphoreType.DMA((8,)),
            pltpu.SemaphoreType.DMA((8,)),
            pltpu.SemaphoreType.DMA((8,)),
            pltpu.SemaphoreType.DMA((12,)),
            pltpu.SemaphoreType.DMA((9,)),
        ],
        compiler_params=pltpu.CompilerParams(
            collective_id=0, has_side_effects=True, vmem_limit_bytes=48 * 2**20
        ),
    )(
        *[
            pltpu.with_memory_space_constraint(value, pltpu.HBM)
            for value in (
                stress,
                velocity,
                buoyancy,
                lame,
                shear,
                fault_tile,
                prestress,
                normal_stress,
                rate_a,
                state,
            )
        ]
    )
    return pl.pallas_call(
        write_kernel,
        out_shape=tuple(jax.ShapeDtypeStruct(value.shape, f32) for value in results),
        in_specs=[vmem] * 4,
        out_specs=(anywhere,) * 4,
        scratch_shapes=[pltpu.SemaphoreType.DMA((11,))],
    )(*[pltpu.with_memory_space_constraint(value, pltpu.VMEM) for value in results])


def solution(mesh):
    in_specs = (
        P(None, "strike", "cross", None),
        P(None, "strike", "cross", None),
        P("strike", "cross", None),
        P("strike", "cross", None),
        P("strike", "cross", None),
        P(),
        P("strike", "cross"),
        P("strike", "cross"),
        P("strike", "cross"),
        P("strike", "cross"),
    )
    out_specs = (
        P(None, "strike", "cross", None),
        P(None, "strike", "cross", None),
        P("strike", "cross"),
        P("strike", "cross"),
    )
    return jax.shard_map(local, mesh=mesh, in_specs=in_specs, out_specs=out_specs, check_vma=False)
```
